256 devices in a mesh: dp: 4 (over x_lo, core), seq: 16 (over x_hi, z), tensor: 4 (over y).
Axes of the slice: x: 4 (x_hi: 2, x_lo: 2; x = x_hi * 2 + x_lo), y: 4, z: 8, core: 2. Of those that a mesh axis runs over, the one named last changes fastest.
Arguments:
- tokens: bfloat16 [12288, 4096], P(('dp', 'seq'), 'tensor'), parts along dimension 0, may hold values from -40 to 40
- input_projection_weight: bfloat16 [4096, 3072], P(None, 'tensor'), may hold values from -0.09375 to 0.09375
- w_out: bfloat16 [2048, 4096], P('tensor'), may hold values from -0.125 to 0.125
- upstream: bfloat16 [12288, 4096], P(('dp', 'seq'), 'tensor'), parts along dimension 0, may hold values from -6 to 6
- exponents: int32 [768, 24], P('dp', 'tensor'), parts along dimension 0, may hold values from -7 to -1
Outputs:
- attended: bfloat16 [12288, 4096], P(('dp', 'seq'), 'tensor'), parts along dimension 0
- grad_tokens: bfloat16 [12288, 4096], P(('dp', 'seq'), 'tensor'), parts along dimension 0
- grad_w_qkv: bfloat16 [16384, 3072], P(('dp', 'seq'), 'tensor'), parts along dimension 0
- grad_w_out: bfloat16 [8192, 4096], P(('dp', 'tensor'), 'seq'), parts along dimension 0
The draws below stay inside these ranges and needn't reach their ends.
There are 4 independent parts, one for each index of `dp`. The reference program is written for one: setup_inputs(seed, part) draws one part's arguments, and reference() takes and returns one part's arrays. A program takes and returns all parts, laid end to end along the dimension named above; an argument that names none is the same for every part. Nothing has to cross between parts.
All inputs are finite; a program needn't handle non-finite values.
Results may differ from the reference program's by a relative error of at most 0.029.
The reference program's roundings to bfloat16 on the way count: a program that leaves them out, or rounds other values in their place, can miss the bound.
Values may be sent and summed in bfloat16 or wider, within the bound.
A program may use at most 128 MiB of HBM per device.

```python
import math
import jax
import jax.numpy as jnp
from jax import lax

MODEL_WIDTH = 4096
HEAD_SIZE = 128
KEY_HEADS = 4
QUERY_PER_KEY = 4
SCALE_TOKENS = 16
TOK_DEV = 192
HQ = 16
TOKEN_COUNT = 3072
N_SEQ = 16
N_TENSOR = 4


def draw_tokens(key, part):
    key = jax.random.fold_in(key, 11)
    first = jax.random.fold_in(key, 0)
    return jnp.clip(jax.random.normal(first, (TOKEN_COUNT, MODEL_WIDTH), jnp.float32), -5.0, 5.0).astype(jnp.bfloat16)


def with_ends(values, stream_key, smallest, largest):
    longest = values.shape.index(max(values.shape))
    spots = []
    for shift in (0, 1):
        where = [jax.random.randint(jax.random.fold_in(stream_key, axis), (), 0, length) for axis, length in enumerate(values.shape)]
        where[longest] = (where[longest] + shift) % values.shape[longest]
        spots.append(tuple(where))
    return values.at[spots[0]].set(smallest).at[spots[1]].set(largest)


def shard_levels(stream_key, extent, pieces, low, high):
    def one(axis_at, parts):
        draws = jax.random.uniform(jax.random.fold_in(jax.random.fold_in(stream_key, 6), axis_at), (parts,), jnp.float32, low / len(pieces), high / len(pieces))
        return jnp.repeat(jnp.exp(draws), extent[axis_at] // parts).reshape((-1,) + (1,) * (len(extent) - axis_at - 1))

    factor_of = one(*pieces[0])
    for cut in pieces[1:]:
        factor_of = factor_of * one(*cut)
    return factor_of


def gaussian(own_key, shape, deviation, bound, cuts=(), held_as=jnp.bfloat16):
    loudness = shard_levels(own_key, shape, cuts, -0.22, 0.18) if cuts else 1.0
    array = jax.random.normal(own_key, shape, jnp.float32) * deviation * loudness
    return jnp.minimum(jnp.maximum(array, -bound), bound).astype(held_as)


def setup_inputs(seed: int = 0, part: int = 0) -> dict:
    splits = jax.random.split(jax.random.key(seed), 6)
    part_splits = jax.random.split(jax.random.fold_in(splits[5], part), 6)
    return {
        "tokens": draw_tokens(jax.random.fold_in(jax.random.fold_in(splits[5], part), 71), part),
        "input_projection_weight": gaussian(splits[1], (MODEL_WIDTH, KEY_HEADS * 6 * HEAD_SIZE), MODEL_WIDTH ** -0.5, 0.09375, ((1, 4),)),
        "w_out": gaussian(splits[2], (HQ * HEAD_SIZE, MODEL_WIDTH), (HQ * HEAD_SIZE) ** -0.5, 0.125, ((0, 4),)),
        "upstream": gaussian(part_splits[3], (TOKEN_COUNT, MODEL_WIDTH), 1.0, 6.0, ((0, 16), (1, 4))),
        "exponents": with_ends(jax.random.randint(part_splits[4], (TOKEN_COUNT // SCALE_TOKENS, KEY_HEADS * 6), -7, 0), jax.random.fold_in(part_splits[4], 1), -7, -1).astype(jnp.int32),
    }


THETA = 500000.0

def rotate(vectors, places, sign):
    half = vectors.shape[-1] // 2
    freqs = jnp.power(jnp.float32(THETA), -jnp.arange(half, dtype=jnp.float32) * 2.0 / vectors.shape[-1])
    angles = places.astype(jnp.float32)[:, None] * freqs[None, :]
    cosine = jnp.cos(angles)[:, None, :]
    sine = sign * jnp.sin(angles)[:, None, :]
    first = vectors[..., :half]
    second = vectors[..., half:]
    return jnp.concatenate([first * cosine - second * sine, second * cosine + first * sine], axis=-1)

def dot_rows(left, right):
    return lax.dot_general(left, right, (((1,), (1,)), ((), ())), preferred_element_type=jnp.float32)

def dot_cols(left, right):
    return lax.dot_general(left, right, (((0,), (0,)), ((), ())), preferred_element_type=jnp.float32)

def forward_block(query, query_places, keys, values, key_places):
    scale = 1.0 / math.sqrt(query.shape[-1])
    scores = dot_rows(query, keys) * scale
    allowed = key_places[None, :] <= query_places[:, None]
    scores = jnp.where(allowed, scores, -jnp.inf)
    top = lax.optimization_barrier(jnp.max(scores, axis=1, keepdims=True))
    weights = jnp.exp(scores - top)
    total = lax.optimization_barrier(jnp.sum(weights, axis=1, keepdims=True))
    mixed = jnp.dot(weights.astype(jnp.bfloat16), values, preferred_element_type=jnp.float32) / total
    return (mixed.astype(jnp.bfloat16), (top + jnp.log(total))[:, 0])

def backward_block(query, query_places, grad_out, output, logsum, keys, values, key_places):
    scale = 1.0 / math.sqrt(query.shape[-1])
    scores = dot_rows(query, keys) * scale
    allowed = key_places[None, :] <= query_places[:, None]
    probs = jnp.exp(jnp.where(allowed, scores - logsum[:, None], -jnp.inf))
    grad_values = dot_cols(probs.astype(jnp.bfloat16), grad_out)
    grad_probs = dot_rows(grad_out, values)
    delta = lax.optimization_barrier(jnp.sum(grad_out.astype(jnp.float32) * output.astype(jnp.float32), axis=1, keepdims=True))
    grad_scores = (probs * (grad_probs - delta)).astype(jnp.bfloat16)
    grad_query = jnp.dot(grad_scores, keys, preferred_element_type=jnp.float32) * scale
    grad_keys = dot_cols(grad_scores, query) * scale
    return (grad_query, grad_keys, grad_values)

def squeeze(gradient, scale_exponent):
    scaled = jnp.clip(gradient * jnp.exp2(-scale_exponent)[..., None], -127.0, 127.0)
    sent = lax.optimization_barrier(scaled.astype(jnp.bfloat16))
    return sent.astype(jnp.float32) * jnp.exp2(scale_exponent)[..., None]

def rounded_sum(terms_left, terms_right, product, shape):

    def add_term(total, couple):
        term = lax.optimization_barrier(product(couple[0], couple[1]).astype(jnp.bfloat16))
        return (total + term.astype(jnp.float32), None)
    return lax.scan(add_term, jnp.zeros(shape, jnp.float32), (terms_left, terms_right))[0]

def reference(tokens, input_projection_weight, w_out, upstream, exponents):
    sequence_length = tokens.shape[0]
    head_layout = QUERY_PER_KEY * KEY_HEADS
    model_width = KEY_HEADS * 6 * HEAD_SIZE
    places = jnp.arange(sequence_length, dtype=jnp.int32)
    projected_rows = jnp.dot(tokens, input_projection_weight, preferred_element_type=jnp.float32).reshape(sequence_length, KEY_HEADS, 6, HEAD_SIZE)
    query = rotate(projected_rows[:, :, :QUERY_PER_KEY].reshape(sequence_length, head_layout, HEAD_SIZE), places, 1.0).astype(jnp.bfloat16)
    keys = rotate(projected_rows[:, :, QUERY_PER_KEY], places, 1.0).astype(jnp.bfloat16)
    values = projected_rows[:, :, QUERY_PER_KEY + 1].astype(jnp.bfloat16)
    block = math.gcd(sequence_length, 512)
    count = sequence_length // block
    block_places = places.reshape(count, block)

    def head_forward(head):
        query_head = lax.dynamic_index_in_dim(query, head, 1, keepdims=False).reshape(count, block, HEAD_SIZE)
        key_head = lax.dynamic_index_in_dim(keys, head // QUERY_PER_KEY, 1, keepdims=False)
        value_head = lax.dynamic_index_in_dim(values, head // QUERY_PER_KEY, 1, keepdims=False)
        return lax.map(lambda blocks: forward_block(blocks[0], blocks[1], key_head, value_head, places), (query_head, block_places))
    outputs, logsums = lax.map(head_forward, jnp.arange(head_layout, dtype=jnp.int32))
    output = outputs.reshape(head_layout, sequence_length, HEAD_SIZE)
    logsum = logsums.reshape(head_layout, sequence_length)
    merged = output.transpose(1, 0, 2).reshape(sequence_length, head_layout * HEAD_SIZE)
    group_cols = head_layout * HEAD_SIZE // N_TENSOR
    attended = rounded_sum(merged.reshape(sequence_length, N_TENSOR, group_cols).transpose(1, 0, 2), w_out.reshape(N_TENSOR, group_cols, MODEL_WIDTH), lambda left, right: jnp.dot(left, right, preferred_element_type=jnp.float32), (sequence_length, MODEL_WIDTH)).astype(jnp.bfloat16)
    grad_merged = dot_rows(upstream, w_out).astype(jnp.bfloat16)
    grad_w_out = rounded_sum(merged.reshape(N_SEQ, TOK_DEV, head_layout * HEAD_SIZE), upstream.reshape(N_SEQ, TOK_DEV, MODEL_WIDTH), dot_cols, (head_layout * HEAD_SIZE, MODEL_WIDTH)).astype(jnp.bfloat16)
    grad_heads = grad_merged.reshape(sequence_length, head_layout, HEAD_SIZE)

    def head_backward(head):
        query_head = lax.dynamic_index_in_dim(query, head, 1, keepdims=False).reshape(count, block, HEAD_SIZE)
        grad_head = lax.dynamic_index_in_dim(grad_heads, head, 1, keepdims=False).reshape(count, block, HEAD_SIZE)
        out_head = lax.dynamic_index_in_dim(output, head, 0, keepdims=False).reshape(count, block, HEAD_SIZE)
        logsum_head = lax.dynamic_index_in_dim(logsum, head, 0, keepdims=False).reshape(count, block)
        key_head = lax.dynamic_index_in_dim(keys, head // QUERY_PER_KEY, 1, keepdims=False)
        value_head = lax.dynamic_index_in_dim(values, head // QUERY_PER_KEY, 1, keepdims=False)

        def step(carry, blocks):
            grad_query, key_gradient, value_gradient = backward_block(blocks[0], blocks[1], blocks[2], blocks[3], blocks[4], key_head, value_head, places)
            return ((carry[0] + key_gradient, carry[1] + value_gradient), grad_query)
        zeros = jnp.zeros((sequence_length, HEAD_SIZE), jnp.float32)
        sums, grad_query = lax.scan(step, (zeros, zeros), (query_head, block_places, grad_head, out_head, logsum_head))
        return (grad_query.reshape(sequence_length, HEAD_SIZE), sums[0], sums[1])
    grad_query, key_gradient, value_gradient = lax.map(head_backward, jnp.arange(head_layout, dtype=jnp.int32))
    key_gradient = key_gradient.reshape(KEY_HEADS, QUERY_PER_KEY, sequence_length, HEAD_SIZE).sum(axis=1)
    value_gradient = value_gradient.reshape(KEY_HEADS, QUERY_PER_KEY, sequence_length, HEAD_SIZE).sum(axis=1)
    scale_exponent = jnp.repeat(exponents.astype(jnp.float32), SCALE_TOKENS, axis=0).reshape(sequence_length, KEY_HEADS, 6)
    query_gradient = rotate(squeeze(grad_query.transpose(1, 0, 2), scale_exponent[:, :, :QUERY_PER_KEY].reshape(sequence_length, head_layout)), places, -1.0).astype(jnp.bfloat16)
    key_rows_gradient = rotate(squeeze(key_gradient.transpose(1, 0, 2), scale_exponent[:, :, QUERY_PER_KEY]), places, -1.0).astype(jnp.bfloat16)
    value_rows_gradient = squeeze(value_gradient.transpose(1, 0, 2), scale_exponent[:, :, QUERY_PER_KEY + 1]).astype(jnp.bfloat16)
    projection_gradient = jnp.concatenate([query_gradient.reshape(sequence_length, KEY_HEADS, QUERY_PER_KEY, HEAD_SIZE), key_rows_gradient[:, :, None], value_rows_gradient[:, :, None]], axis=2).reshape(sequence_length, model_width)
    part_cols = model_width // N_TENSOR
    grad_tokens = rounded_sum(projection_gradient.reshape(sequence_length, N_TENSOR, part_cols).transpose(1, 0, 2), input_projection_weight.reshape(MODEL_WIDTH, N_TENSOR, part_cols).transpose(1, 0, 2), dot_rows, (sequence_length, MODEL_WIDTH)).astype(jnp.bfloat16)
    grad_w_qkv = rounded_sum(tokens.reshape(N_SEQ, TOK_DEV, MODEL_WIDTH), projection_gradient.reshape(N_SEQ, TOK_DEV, model_width), dot_cols, (MODEL_WIDTH, model_width)).astype(jnp.bfloat16)
    return (attended, grad_tokens, grad_w_qkv, grad_w_out)
```

```python
import functools
import math

import jax
import jax.numpy as jnp
from jax import lax
from jax.experimental import pallas as pl
from jax.experimental.pallas import tpu as pltpu
from jax.sharding import PartitionSpec as P

HEAD_SIZE = 128
QUERY_PER_KEY = 4
SCALE_TOKENS = 16
THETA = 500000.0

NZ = 8
NT = 4
ROWS = 192
QROWS = QUERY_PER_KEY * ROWS
CHUNK = 256
WIDTH = 1024
MESH = pl.DeviceIdType.MESH
BF16 = jnp.bfloat16
F32 = jnp.float32
SCALE = 1.0 / math.sqrt(HEAD_SIZE)
SCALE2 = SCALE * math.log2(math.e)
VMEM_LIMIT = 60 * 2**20


def dot(left, right, left_dim, right_dim):
    return lax.dot_general(
        left, right, (((left_dim,), (right_dim,)), ((), ())), preferred_element_type=F32
    )


class Place:
    def __init__(self):
        self.d = lax.axis_index("dp")
        self.s = lax.axis_index("seq")
        self.t = lax.axis_index("tensor")
        self.xh = lax.div(self.s, NZ)
        self.z = lax.rem(self.s, NZ)

    def tensor(self, offset):
        return (self.d, self.s, lax.rem(self.t + offset, NT))

    def zdev(self, sign):
        return (self.d, self.xh * NZ + lax.rem(self.z + sign + NZ, NZ), self.t)

    def xdev(self):
        return (self.d, (1 - self.xh) * NZ + self.z, self.t)

    def enter(self):
        barrier = pltpu.get_barrier_semaphore()
        partners = [self.tensor(1), self.tensor(2), self.tensor(3)]
        partners += [self.zdev(1), self.zdev(-1), self.xdev()]
        for partner in partners:
            pl.semaphore_signal(barrier, inc=1, device_id=partner, device_id_type=MESH)
        pl.semaphore_wait(barrier, len(partners))


def remote(src, dst, send_sem, recv_sem, device):
    return pltpu.make_async_remote_copy(
        src_ref=src,
        dst_ref=dst,
        send_sem=send_sem,
        recv_sem=recv_sem,
        device_id=device,
        device_id_type=MESH,
    )


def turn(vectors, cosine, sine):
    return vectors * cosine + pltpu.roll(vectors, HEAD_SIZE // 2, 1) * sine


def gather_column(place, kv, column, which, ss, rs, sends):
    def block(z):
        return kv.at[column * NZ + lax.rem(z + 2 * NZ, NZ)]

    def part(step, di, ref):
        return ref.at[pl.ds(di * ROWS, ROWS)] if step == 4 else ref

    def arrived(step, di, sign):
        ref = part(step, di, block(place.z - sign * step))
        sem = rs.at[which, di, step - 1]
        remote(ref, ref, ss.at[which, di, step - 1], sem, place.zdev(sign)).wait_recv()

    for step in range(1, 5):
        for di, sign in ((0, 1), (1, -1)):
            if step > 1:
                arrived(step - 1, di, sign)
            ref = part(step, di, block(place.z - sign * (step - 1)))
            copy = remote(
                ref,
                ref,
                ss.at[which, di, step - 1],
                rs.at[which, di, step - 1],
                place.zdev(sign),
            )
            copy.start()
            sends.append(copy)
        yield
    for di, sign in ((0, 1), (1, -1)):
        arrived(4, di, sign)


def scatter_ring(place, subs, rows, load, sbuf, rbuf, ss, rs, sends, done):
    half = rows // 2
    for step in (4, 3, 2, 1):
        for sub in range(subs):
            for di, sign in ((0, 1), (1, -1)):
                dest = lax.rem(place.z + sign * step + NZ, NZ)
                cut = pl.ds(di * half, half)
                here = sbuf.at[di, step - 1, sub]
                there = rbuf.at[di, step - 1, sub]
                if step == 4:
                    here, there = here.at[cut], there.at[cut]
                    here[...] = load(dest, sub, di).astype(BF16)
                else:
                    value = load(dest, sub, None)
                    before = rbuf.at[di, step, sub]
                    if step == 3:
                        before = before.at[cut]
                    remote(
                        before, before, ss.at[di, step, sub], rs.at[di, step, sub], place.zdev(sign)
                    ).wait_recv()
                    if step == 3:
                        here[cut] = (value[di * half : (di + 1) * half] + before[...]).astype(BF16)
                        rest = 1 - di
                        here[pl.ds(rest * half, half)] = value[
                            rest * half : (rest + 1) * half
                        ].astype(BF16)
                    else:
                        here[...] = (value + before[...]).astype(BF16)
                copy = remote(
                    here, there, ss.at[di, step - 1, sub], rs.at[di, step - 1, sub], place.zdev(sign)
                )
                copy.start()
                sends.append(copy)
            yield
    for sub in range(subs):
        total = load(place.z, sub, None)
        for di, sign in ((0, 1), (1, -1)):
            ref = rbuf.at[di, 0, sub]
            remote(ref, ref, ss.at[di, 0, sub], rs.at[di, 0, sub], place.zdev(sign)).wait_recv()
            total = total + ref[...]
        done(sub, total)


def run(steps, count=None):
    if count is None:
        for _ in steps:
            pass
    else:
        for _ in range(count):
            next(steps)


def project_kernel(
    tok, up, wq_hbm, wo_hbm, cosine, sine,
    q_out, kv, do_out, tok_all, up_all, tok_other,
    wq, wo, load_sem, tok_ss, tok_rs, up_ss, up_rs, x_ss, x_rs, kv_ss, kv_rs,
):
    place = Place()
    t = place.t
    loads = []
    for i in range(NT):
        rows = pl.ds(pl.multiple_of(lax.rem(t + (0, 1, 3, 2)[i], NT) * WIDTH, WIDTH), WIDTH)
        loads.append(pltpu.make_async_copy(wq_hbm.at[rows], wq.at[rows], load_sem.at[i]))
        loads[-1].start()
    load_wo = pltpu.make_async_copy(wo_hbm, wo, load_sem.at[4])
    load_wo.start()
    place.enter()
    sends = []

    def spread(own, everyone, ss, rs):
        for offset in (1, 3, 2):
            copy = remote(
                own, everyone.at[t], ss.at[offset - 1], rs.at[offset - 1], place.tensor(offset)
            )
            copy.start()
            sends.append(copy)

    def arrived(everyone, offset, ss, rs):
        source = lax.rem(t + NT - offset, NT)
        ref = everyone.at[source]
        remote(ref, ref, ss.at[offset - 1], rs.at[offset - 1], place.tensor(offset)).wait_recv()
        return source

    spread(tok, tok_all, tok_ss, tok_rs)
    tok_all[t] = tok[...]
    up_all[t] = up[...]
    loads[0].wait()
    acc = dot(tok[...], wq[pl.ds(pl.multiple_of(t * WIDTH, WIDTH), WIDTH)], 1, 0)
    for load in loads[1:]:
        load.wait()
    for offset in (1, 3, 2):
        source = arrived(tok_all, offset, tok_ss, tok_rs)
        rows = pl.ds(pl.multiple_of(source * WIDTH, WIDTH), WIDTH)
        if offset == 2:
            for copy in sends:
                copy.wait_send()
            sends.clear()
            spread(up, up_all, up_ss, up_rs)
        acc = acc + dot(tok_all[source], wq[rows], 1, 0)

    c, s = cosine[...], sine[...]
    kv[place.s, pl.ds(0, ROWS)] = turn(acc[:, 512:640], c, s).astype(BF16)
    kv[place.s, pl.ds(ROWS, ROWS)] = acc[:, 640:768].astype(BF16)
    x_kv = remote(kv.at[place.s], kv.at[place.s], x_ss.at[0], x_rs.at[0], place.xdev())
    x_kv.start()
    mine = gather_column(place, kv, place.xh, 0, kv_ss, kv_rs, sends)
    run(mine, 1)
    for h in range(QUERY_PER_KEY):
        q_out[pl.ds(h * ROWS, ROWS)] = turn(
            acc[:, h * HEAD_SIZE : (h + 1) * HEAD_SIZE], c, s
        ).astype(BF16)
    other = (1 - place.xh) * NZ + place.z
    remote(kv.at[other], kv.at[other], x_ss.at[0], x_rs.at[0], place.xdev()).wait_recv()
    sends.append(x_kv)
    theirs = gather_column(place, kv, 1 - place.xh, 1, kv_ss, kv_rs, sends)
    run(theirs, 1)
    x_tok = []
    for i in range(2):
        copy = remote(
            tok_all.at[2 * (1 - place.xh) + i],
            tok_other.at[i],
            x_ss.at[1 + i],
            x_rs.at[1 + i],
            place.xdev(),
        )
        copy.start()
        x_tok.append(copy)
    run(mine, 1)
    run(theirs, 1)
    load_wo.wait()

    def merged_term(source):
        columns = pl.ds(pl.multiple_of(source * WIDTH, WIDTH), WIDTH)
        return dot(up_all[source], wo[:, columns], 1, 1)

    grad = merged_term(t)
    grad = grad + merged_term(arrived(up_all, 1, up_ss, up_rs))
    run(mine, 1)
    run(theirs, 1)
    grad = grad + merged_term(arrived(up_all, 3, up_ss, up_rs))
    run(mine, 1)
    run(theirs, 1)
    grad = grad + merged_term(arrived(up_all, 2, up_ss, up_rs))
    for h in range(QUERY_PER_KEY):
        do_out[pl.ds(h * ROWS, ROWS)] = grad[:, h * HEAD_SIZE : (h + 1) * HEAD_SIZE].astype(BF16)
    run(mine)
    run(theirs)
    for copy in x_tok:
        copy.wait()
    for copy in sends:
        copy.wait_send()


def project(tok, up, wq, wo, cosine, sine):
    vmem = pl.BlockSpec(memory_space=pltpu.VMEM)
    hbm = pl.BlockSpec(memory_space=pl.ANY)
    shape = jax.ShapeDtypeStruct
    dma = pltpu.SemaphoreType.DMA
    return pl.pallas_call(
        project_kernel,
        name="project",
        out_shape=[
            shape((QROWS, HEAD_SIZE), BF16),
            shape((2 * NZ, 2 * ROWS, HEAD_SIZE), BF16),
            shape((QROWS, HEAD_SIZE), BF16),
            shape((NT, ROWS, WIDTH), BF16),
            shape((NT, ROWS, WIDTH), BF16),
            shape((2, ROWS, WIDTH), BF16),
        ],
        in_specs=[vmem, vmem, hbm, hbm, vmem, vmem],
        out_specs=[vmem] * 6,
        scratch_shapes=[
            pltpu.VMEM(wq.shape, BF16),
            pltpu.VMEM(wo.shape, BF16),
            dma((5,)),
            dma((3,)),
            dma((3,)),
            dma((3,)),
            dma((3,)),
            dma((3,)),
            dma((3,)),
            dma((2, 2, 4)),
            dma((2, 2, 4)),
        ],
        compiler_params=pltpu.CompilerParams(
            collective_id=0, has_side_effects=True, vmem_limit_bytes=VMEM_LIMIT
        ),
    )(tok, up, wq, wo, cosine, sine)


def attend_kernel(
    q, kv, do, cosine, sine, expo,
    merged, gq, dkv,
    top, total, acc, logsum, delta, dq,
):
    s = lax.axis_index("seq")
    chunks = [pl.ds(c * CHUNK, CHUNK) for c in range(QROWS // CHUNK)]
    top[...] = jnp.full(top.shape, -1e30, F32)
    total[...] = jnp.zeros(total.shape, F32)
    acc[...] = jnp.zeros(acc.shape, F32)
    dq[...] = jnp.zeros(dq.shape, F32)

    def allowed(c):
        key = lax.broadcasted_iota(jnp.int32, (ROWS, CHUNK), 0)
        query = lax.broadcasted_iota(jnp.int32, (ROWS, CHUNK), 1) + c * CHUNK
        return key <= lax.rem(query, ROWS)

    def forward(j, masked):
        keys = kv[j, pl.ds(0, ROWS)]
        values = kv[j, pl.ds(ROWS, ROWS)]
        for c, cut in enumerate(chunks):
            scores = dot(keys, q[cut], 1, 1)
            if masked:
                scores = jnp.where(allowed(c), scores, -jnp.inf)
            before = top[:, cut]
            now = jnp.maximum(before, jnp.max(scores, axis=0, keepdims=True))
            weights = jnp.exp2((scores - now) * SCALE2)
            alpha = jnp.exp2((before - now) * SCALE2)
            top[:, cut] = now
            total[:, cut] = total[:, cut] * alpha + jnp.sum(weights, axis=0, keepdims=True)
            acc[:, cut] = acc[:, cut] * alpha + dot(values, weights.astype(BF16), 0, 0)

    @pl.loop(0, s)
    def _(j):
        forward(j, False)

    forward(s, True)
    out_t = (acc[...] / total[...]).astype(BF16)
    logsum[...] = top[...] * SCALE2 + jnp.log2(total[...])
    do_t = do[...].astype(F32).T
    delta[...] = jnp.sum(do_t * out_t.astype(F32), axis=0, keepdims=True)
    out = out_t.astype(F32).T.astype(BF16)
    for h in range(QUERY_PER_KEY):
        merged[:, h * HEAD_SIZE : (h + 1) * HEAD_SIZE] = out[h * ROWS : (h + 1) * ROWS]

    def backward(j, masked):
        keys = kv[j, pl.ds(0, ROWS)]
        values = kv[j, pl.ds(ROWS, ROWS)]
        dk = jnp.zeros((ROWS, HEAD_SIZE), F32)
        dv = jnp.zeros((ROWS, HEAD_SIZE), F32)
        for c, cut in enumerate(chunks):
            scores = dot(keys, q[cut], 1, 1)
            probs = jnp.exp2(scores * SCALE2 - logsum[:, cut])
            if masked:
                probs = jnp.where(allowed(c), probs, 0.0)
            grad_probs = dot(values, do[cut], 1, 1)
            grad_scores = (probs * (grad_probs - delta[:, cut])).astype(BF16)
            dv = dv + dot(probs.astype(BF16), do[cut], 1, 0)
            dk = dk + dot(grad_scores, q[cut], 1, 0)
            dq[:, cut] += dot(keys, grad_scores, 0, 0)
        dkv[j, pl.ds(0, ROWS)] = (dk * SCALE).astype(BF16)
        dkv[j, pl.ds(ROWS, ROWS)] = dv.astype(BF16)

    @pl.loop(0, s)
    def _(j):
        backward(j, False)

    backward(s, True)

    @pl.loop(s + 1, 2 * NZ)
    def _(j):
        dkv[j] = jnp.zeros((2 * ROWS, HEAD_SIZE), BF16)

    grad = dq[...].T * SCALE
    c, s_ = cosine[...], sine[...]
    for h in range(QUERY_PER_KEY):
        e = expo[:, h : h + 1]
        sent = jnp.clip(grad[h * ROWS : (h + 1) * ROWS] * jnp.exp2(-e), -127.0, 127.0).astype(BF16)
        gq[:, h * HEAD_SIZE : (h + 1) * HEAD_SIZE] = turn(
            sent.astype(F32) * jnp.exp2(e), c, -s_
        ).astype(BF16)


def attend(q, kv, do, cosine, sine, expo):
    vmem = pl.BlockSpec(memory_space=pltpu.VMEM)
    shape = jax.ShapeDtypeStruct
    return pl.pallas_call(
        attend_kernel,
        name="attend",
        out_shape=[
            shape((ROWS, QUERY_PER_KEY * HEAD_SIZE), BF16),
            shape((ROWS, QUERY_PER_KEY * HEAD_SIZE), BF16),
            shape((2 * NZ, 2 * ROWS, HEAD_SIZE), BF16),
        ],
        in_specs=[vmem] * 6,
        out_specs=[vmem] * 3,
        scratch_shapes=[
            pltpu.VMEM((1, QROWS), F32),
            pltpu.VMEM((1, QROWS), F32),
            pltpu.VMEM((HEAD_SIZE, QROWS), F32),
            pltpu.VMEM((1, QROWS), F32),
            pltpu.VMEM((1, QROWS), F32),
            pltpu.VMEM((HEAD_SIZE, QROWS), F32),
        ],
        compiler_params=pltpu.CompilerParams(vmem_limit_bytes=VMEM_LIMIT),
    )(q, kv, do, cosine, sine, expo)


def finish_kernel(
    merged, gq, dkv, tok_all, up_all, tok_other, wq_hbm, wo_hbm, cosine, sine, expo,
    attended, grad_tokens, gwq, gwo,
    wq, wo, merged_other, up_other, gqkv, kv_own, kv_out, kv_in,
    att_own, att_s, att_r, tok_own, tok_s, tok_r,
    kv_sb, kv_rb, o_sb, o_rb, q_sb, q_rb,
    load_sem, x_ss, x_rs, y_ss, y_rs, kv_ss, kv_rs, o_ss, o_rs, q_ss, q_rs,
):
    place = Place()
    t, xh = place.t, place.xh
    load_wo = pltpu.make_async_copy(wo_hbm, wo, load_sem.at[0])
    load_wo.start()
    load_wq = pltpu.make_async_copy(wq_hbm, wq, load_sem.at[1])
    load_wq.start()
    place.enter()
    sends = []

    def swap(src, dst, i):
        copy = remote(src, dst, x_ss.at[i], x_rs.at[i], place.xdev())
        copy.start()
        return copy

    x_merged = swap(merged, merged_other, 0)
    x_up = [swap(up_all.at[2 * (1 - xh) + i], up_other.at[i], 1 + i) for i in range(2)]

    def load_kv(dest, sub, part):
        ref = dkv.at[((1 - xh) if sub == 0 else xh) * NZ + dest]
        if part is not None:
            return ref[pl.ds(part * ROWS, ROWS)].astype(F32)
        return ref[...].astype(F32)

    def done_kv(sub, value):
        if sub == 0:
            kv_out[...] = value.astype(BF16)
        else:
            kv_own[...] = value

    ring_kv = scatter_ring(
        place, 2, 2 * ROWS, load_kv, kv_sb, kv_rb, kv_ss, kv_rs, sends, done_kv
    )
    run(ring_kv, 2)

    def scatter_tensor(term, own, sbuf, rbuf, which):
        for offset in (1, 3, 2):
            sbuf[offset - 1] = term(lax.rem(t + offset, NT)).astype(BF16)
            copy = remote(
                sbuf.at[offset - 1],
                rbuf.at[offset - 1],
                y_ss.at[which, offset - 1],
                y_rs.at[which, offset - 1],
                place.tensor(offset),
            )
            copy.start()
            sends.append(copy)
        own[...] = term(t)

    def collect_tensor(own, rbuf, which, out):
        value = own[...]
        for offset in (1, 3, 2):
            ref = rbuf.at[offset - 1]
            remote(
                ref,
                ref,
                y_ss.at[which, offset - 1],
                y_rs.at[which, offset - 1],
                place.tensor(offset),
            ).wait_recv()
            value = value + ref[...]
        out[...] = value.astype(BF16)

    def attended_term(dest):
        return dot(merged[...], wo[:, pl.ds(pl.multiple_of(dest * WIDTH, WIDTH), WIDTH)], 1, 0)

    def tokens_term(dest):
        return dot(gqkv[0], wq[pl.ds(pl.multiple_of(dest * WIDTH, WIDTH), WIDTH)], 1, 1)

    load_wo.wait()
    scatter_tensor(attended_term, att_own, att_s, att_r, 0)
    run(ring_kv)
    x_kv = swap(kv_out, kv_in, 3)
    c, s = cosine[...], sine[...]
    gqkv[0, :, 0:512] = gq[...]
    x_kv.wait()
    grad = kv_own[...] + kv_in[...]

    def squeeze(value, column):
        e = expo[:, column : column + 1]
        sent = jnp.clip(value * jnp.exp2(-e), -127.0, 127.0).astype(BF16)
        return sent.astype(F32) * jnp.exp2(e)

    gqkv[0, :, 512:640] = turn(squeeze(grad[:ROWS], 4), c, -s).astype(BF16)
    gqkv[0, :, 640:768] = squeeze(grad[ROWS:], 5).astype(BF16)
    x_gqkv = swap(gqkv.at[0], gqkv.at[1], 4)
    load_wq.wait()
    scatter_tensor(tokens_term, tok_own, tok_s, tok_r, 1)

    def columns(dest):
        return pl.ds(pl.multiple_of(lax.rem(dest, 4) * 256, 256), 256)

    def load_o(dest, sub, part):
        first = sub * 256 + (0 if part is None else part * 128)
        last = first + (256 if part is None else 128)
        shard = lax.div(dest, 4)
        value = dot(merged[:, first:last], up_all[2 * xh + shard, :, columns(dest)], 0, 0)
        return value + dot(
            merged_other[:, first:last], up_other[shard, :, columns(dest)], 0, 0
        )

    def done_o(sub, value):
        gwo[pl.ds(sub * 256, 256)] = value.astype(BF16)

    def load_q(dest, sub, part):
        shard = lax.div(dest, 4)
        left = tok_all[2 * xh + shard, :, columns(dest)]
        left_other = tok_other[shard, :, columns(dest)]
        if part is not None:
            left = left[:, part * 128 : (part + 1) * 128]
            left_other = left_other[:, part * 128 : (part + 1) * 128]
        cut = slice(sub * 256, (sub + 1) * 256)
        return dot(left, gqkv[0, :, cut], 0, 0) + dot(left_other, gqkv[1, :, cut], 0, 0)

    def done_q(sub, value):
        gwq[:, sub * 256 : (sub + 1) * 256] = value.astype(BF16)

    x_merged.wait()
    for copy in x_up:
        copy.wait()
    ring_o = scatter_ring(place, 2, 256, load_o, o_sb, o_rb, o_ss, o_rs, sends, done_o)
    ring_q = scatter_ring(place, 3, 256, load_q, q_sb, q_rb, q_ss, q_rs, sends, done_q)
    run(ring_o, 6)
    x_gqkv.wait()
    run(ring_q, 3)
    run(ring_o)
    collect_tensor(att_own, att_r, 0, attended)
    run(ring_q, 6)
    collect_tensor(tok_own, tok_r, 1, grad_tokens)
    run(ring_q)
    for copy in sends:
        copy.wait_send()


def finish(merged, gq, dkv, tok_all, up_all, tok_other, wq, wo, cosine, sine, expo):
    vmem = pl.BlockSpec(memory_space=pltpu.VMEM)
    hbm = pl.BlockSpec(memory_space=pl.ANY)
    shape = jax.ShapeDtypeStruct
    dma = pltpu.SemaphoreType.DMA
    ring = pltpu.VMEM
    return pl.pallas_call(
        finish_kernel,
        name="finish",
        out_shape=[
            shape((ROWS, WIDTH), BF16),
            shape((ROWS, WIDTH), BF16),
            shape((256, 768), BF16),
            shape((512, 256), BF16),
        ],
        in_specs=[vmem] * 6 + [hbm] * 2 + [vmem] * 3,
        out_specs=[vmem] * 4,
        scratch_shapes=[
            pltpu.VMEM(wq.shape, BF16),
            pltpu.VMEM(wo.shape, BF16),
            pltpu.VMEM((ROWS, 512), BF16),
            pltpu.VMEM((2, ROWS, WIDTH), BF16),
            pltpu.VMEM((2, ROWS, 768), BF16),
            pltpu.VMEM((2 * ROWS, HEAD_SIZE), F32),
            pltpu.VMEM((2 * ROWS, HEAD_SIZE), BF16),
            pltpu.VMEM((2 * ROWS, HEAD_SIZE), BF16),
            pltpu.VMEM((ROWS, WIDTH), F32),
            pltpu.VMEM((3, ROWS, WIDTH), BF16),
            pltpu.VMEM((3, ROWS, WIDTH), BF16),
            pltpu.VMEM((ROWS, WIDTH), F32),
            pltpu.VMEM((3, ROWS, WIDTH), BF16),
            pltpu.VMEM((3, ROWS, WIDTH), BF16),
            ring((2, 4, 2, 2 * ROWS, HEAD_SIZE), BF16),
            ring((2, 4, 2, 2 * ROWS, HEAD_SIZE), BF16),
            ring((2, 4, 2, 256, 256), BF16),
            ring((2, 4, 2, 256, 256), BF16),
            ring((2, 4, 3, 256, 256), BF16),
            ring((2, 4, 3, 256, 256), BF16),
            dma((2,)),
            dma((5,)),
            dma((5,)),
            dma((2, 3)),
            dma((2, 3)),
            dma((2, 4, 2)),
            dma((2, 4, 2)),
            dma((2, 4, 2)),
            dma((2, 4, 2)),
            dma((2, 4, 3)),
            dma((2, 4, 3)),
        ],
        compiler_params=pltpu.CompilerParams(
            collective_id=1, has_side_effects=True, vmem_limit_bytes=VMEM_LIMIT
        ),
    )(merged, gq, dkv, tok_all, up_all, tok_other, wq, wo, cosine, sine, expo)


def local(tokens, input_projection_weight, w_out, upstream, exponents):
    seq_index = lax.axis_index("seq")
    half = HEAD_SIZE // 2
    freqs = jnp.power(F32(THETA), -jnp.arange(half, dtype=F32) * 2.0 / HEAD_SIZE)
    places = seq_index * ROWS + jnp.arange(ROWS, dtype=jnp.int32)
    angles = places.astype(F32)[:, None] * freqs[None, :]
    cosine = jnp.tile(jnp.cos(angles), (1, 2))
    sine = jnp.sin(angles)
    sine = jnp.concatenate([-sine, sine], axis=1)
    groups = ROWS // SCALE_TOKENS
    mine = lax.dynamic_slice_in_dim(exponents, seq_index * groups, groups, 0).astype(F32)
    expo = jnp.repeat(mine, SCALE_TOKENS, axis=0)
    q, kv, do, tok_all, up_all, tok_other = project(
        tokens, upstream, input_projection_weight, w_out, cosine, sine
    )
    merged, gq, dkv = attend(q, kv, do, cosine, sine, expo)
    return finish(
        merged,
        gq,
        dkv,
        tok_all,
        up_all,
        tok_other,
        input_projection_weight,
        w_out,
        cosine,
        sine,
        expo,
    )


def solution(mesh):
    in_specs = (
        P(("dp", "seq"), "tensor"),
        P(None, "tensor"),
        P("tensor", None),
        P(("dp", "seq"), "tensor"),
        P("dp", "tensor"),
    )
    out_specs = (
        P(("dp", "seq"), "tensor"),
        P(("dp", "seq"), "tensor"),
        P(("dp", "seq"), "tensor"),
        P(("dp", "tensor"), "seq"),
    )
    return jax.shard_map(local, mesh=mesh, in_specs=in_specs, out_specs=out_specs, check_vma=False)
```

```python
import functools
import math

import jax
import jax.numpy as jnp
from jax import lax
from jax.experimental import pallas as pl
from jax.experimental.pallas import tpu as pltpu
from jax.sharding import PartitionSpec as P

HEAD_SIZE = 128
QUERY_PER_KEY = 4
SCALE_TOKENS = 16
THETA = 500000.0

NZ = 8
NT = 4
ROWS = 192
QROWS = QUERY_PER_KEY * ROWS
PAIR = 2 * ROWS
WIDTH = 1024
MESH = pl.DeviceIdType.MESH
BF16 = jnp.bfloat16
F32 = jnp.float32
SCALE = 1.0 / math.sqrt(HEAD_SIZE)
SCALE2 = SCALE * math.log2(math.e)
VMEM_LIMIT = 60 * 2**20


def dot(left, right, left_dim, right_dim):
    return lax.dot_general(
        left, right, (((left_dim,), (right_dim,)), ((), ())), preferred_element_type=F32
    )


class Place:
    def __init__(self):
        self.d = lax.axis_index("dp")
        self.s = lax.axis_index("seq")
        self.t = lax.axis_index("tensor")
        self.xh = lax.div(self.s, NZ)
        self.z = lax.rem(self.s, NZ)

    def tensor(self, offset):
        return (self.d, self.s, lax.rem(self.t + offset, NT))

    def zdev(self, sign):
        return (self.d, self.xh * NZ + lax.rem(self.z + sign + NZ, NZ), self.t)

    def xdev(self):
        return (self.d, (1 - self.xh) * NZ + self.z, self.t)

    def enter(self):
        barrier = pltpu.get_barrier_semaphore()
        partners = [self.tensor(1), self.tensor(2), self.tensor(3)]
        partners += [self.zdev(1), self.zdev(-1), self.xdev()]
        for partner in partners:
            pl.semaphore_signal(barrier, inc=1, device_id=partner, device_id_type=MESH)
        pl.semaphore_wait(barrier, len(partners))


def remote(src, dst, send_sem, recv_sem, device):
    return pltpu.make_async_remote_copy(
        src_ref=src,
        dst_ref=dst,
        send_sem=send_sem,
        recv_sem=recv_sem,
        device_id=device,
        device_id_type=MESH,
    )


def turn(vectors, cosine, sine):
    return vectors * cosine + pltpu.roll(vectors, HEAD_SIZE // 2, 1) * sine


def gather_column(place, kv, column, which, ss, rs, sends):
    cut = pl.ds(pl.multiple_of(column * ROWS, ROWS), ROWS)

    def part(step, di, z):
        z = lax.rem(z + 2 * NZ, NZ)
        return kv.at[di, z, cut] if step == 4 else kv.at[:, z, cut]

    def arrived(step, di, sign):
        ref = part(step, di, place.z - sign * step)
        sem = rs.at[which, di, step - 1]
        remote(ref, ref, ss.at[which, di, step - 1], sem, place.zdev(sign)).wait_recv()

    for step in range(1, 5):
        for di, sign in ((0, 1), (1, -1)):
            if step > 1:
                arrived(step - 1, di, sign)
            ref = part(step, di, place.z - sign * (step - 1))
            copy = remote(
                ref,
                ref,
                ss.at[which, di, step - 1],
                rs.at[which, di, step - 1],
                place.zdev(sign),
            )
            copy.start()
            sends.append(copy)
        yield
    for di, sign in ((0, 1), (1, -1)):
        arrived(4, di, sign)


def scatter_ring(place, subs, rows, load, sbuf, rbuf, ss, rs, sends, done):
    half = rows // 2
    for step in (4, 3, 2, 1):
        for sub in subs:
            for di, sign in ((0, 1), (1, -1)):
                dest = lax.rem(place.z + sign * step + NZ, NZ)
                cut = pl.ds(di * half, half)
                here = sbuf.at[di, step - 1, sub]
                there = rbuf.at[di, step - 1, sub]
                if step == 4:
                    here, there = here.at[cut], there.at[cut]
                    here[...] = load(dest, sub, di).astype(BF16)
                else:
                    value = load(dest, sub, None)
                    before = rbuf.at[di, step, sub]
                    if step == 3:
                        before = before.at[cut]
                    remote(
                        before, before, ss.at[di, step, sub], rs.at[di, step, sub], place.zdev(sign)
                    ).wait_recv()
                    if step == 3:
                        here[cut] = (value[di * half : (di + 1) * half] + before[...]).astype(BF16)
                        rest = 1 - di
                        here[pl.ds(rest * half, half)] = value[
                            rest * half : (rest + 1) * half
                        ].astype(BF16)
                    else:
                        here[...] = (value + before[...]).astype(BF16)
                copy = remote(
                    here, there, ss.at[di, step - 1, sub], rs.at[di, step - 1, sub], place.zdev(sign)
                )
                copy.start()
                sends.append(copy)
            yield
    for sub in subs:
        total = load(place.z, sub, None)
        for di, sign in ((0, 1), (1, -1)):
            ref = rbuf.at[di, 0, sub]
            remote(ref, ref, ss.at[di, 0, sub], rs.at[di, 0, sub], place.zdev(sign)).wait_recv()
            total = total + ref[...]
        done(sub, total)


def run(steps, count=None):
    if count is None:
        for _ in steps:
            pass
    else:
        for _ in range(count):
            next(steps)


def layer_kernel(
    tok, up, wq_hbm, wo_hbm, freqs, exponents,
    attended, grad_tokens, gwq, gwo,
    wq, wo, tok_all, up_all, tok_other, up_other, cosine, sine, expo,
    q, kv, do, merged, merged_other, gqkv,
    key_place, limit, top, total, acc, logsum, delta, dq,
    dkv, kv_own, kv_out, kv_in,
    att_own, att_s, att_r, tok_own, tok_s, tok_r,
    kv_sb, kv_rb, o_sb, o_rb, q_sb, q_rb,
    load_sem, y_ss, y_rs, x_ss, x_rs, ag_ss, ag_rs,
    kv_ss, kv_rs, o_ss, o_rs, q_ss, q_rs,
):
    place = Place()
    t, xh, z = place.t, place.xh, place.z
    loads = []
    for i in range(NT):
        rows = pl.ds(pl.multiple_of(lax.rem(t + (0, 1, 3, 2)[i], NT) * WIDTH, WIDTH), WIDTH)
        loads.append(pltpu.make_async_copy(wq_hbm.at[rows], wq.at[rows], load_sem.at[i]))
        loads[-1].start()
    load_wo = pltpu.make_async_copy(wo_hbm, wo, load_sem.at[4])
    load_wo.start()
    place.enter()
    sends = []

    def swap(src, dst, i):
        copy = remote(src, dst, x_ss.at[i], x_rs.at[i], place.xdev())
        copy.start()
        return copy

    def spread(own, everyone, which):
        copies = []
        for offset in (1, 3, 2):
            copy = remote(
                own,
                everyone.at[t],
                y_ss.at[which, offset - 1],
                y_rs.at[which, offset - 1],
                place.tensor(offset),
            )
            copy.start()
            copies.append(copy)
        return copies

    def arrived(everyone, offset, which):
        source = lax.rem(t + NT - offset, NT)
        ref = everyone.at[source]
        remote(
            ref, ref, y_ss.at[which, offset - 1], y_rs.at[which, offset - 1], place.tensor(offset)
        ).wait_recv()
        return source

    def scatter_tensor(term, own, sbuf, rbuf, which):
        for offset in (1, 3, 2):
            sbuf[offset - 1] = term(lax.rem(t + offset, NT)).astype(BF16)
            copy = remote(
                sbuf.at[offset - 1],
                rbuf.at[offset - 1],
                y_ss.at[which, offset - 1],
                y_rs.at[which, offset - 1],
                place.tensor(offset),
            )
            copy.start()
            sends.append(copy)
        own[...] = term(t)

    def collect_tensor(own, rbuf, which, out):
        value = own[...]
        for offset in (1, 3, 2):
            ref = rbuf.at[offset - 1]
            remote(
                ref,
                ref,
                y_ss.at[which, offset - 1],
                y_rs.at[which, offset - 1],
                place.tensor(offset),
            ).wait_recv()
            value = value + ref[...]
        out[...] = value.astype(BF16)

    token_sends = spread(tok, tok_all, 0)
    tok_all[t] = tok[...]
    up_all[t] = up[...]
    position = lax.broadcasted_iota(jnp.int32, (ROWS, HEAD_SIZE), 0) + place.s * ROWS
    angles = position.astype(F32) * freqs[...]
    cosine[...] = jnp.cos(angles)
    low = lax.broadcasted_iota(jnp.int32, (ROWS, HEAD_SIZE), 1) < HEAD_SIZE // 2
    sines = jnp.sin(angles)
    sine[...] = jnp.where(low, -sines, sines)
    groups = exponents.shape[0]
    group = lax.broadcasted_iota(jnp.int32, (ROWS, groups), 0) // SCALE_TOKENS
    group = group + place.s * (ROWS // SCALE_TOKENS)
    pick = lax.broadcasted_iota(jnp.int32, (ROWS, groups), 1) == group
    expo[...] = dot(pick.astype(F32).astype(BF16), exponents[...].astype(F32).astype(BF16), 1, 0)
    row = lax.broadcasted_iota(jnp.int32, (PAIR, HEAD_SIZE), 0)
    key_place[...] = jnp.where(row < ROWS, row, row + (NZ - 1) * ROWS)
    limit[...] = place.s * ROWS + lax.rem(
        lax.broadcasted_iota(jnp.int32, (1, QROWS), 1), jnp.int32(ROWS)
    )
    top[...] = jnp.full(top.shape, -jnp.inf, F32)
    total[...] = jnp.zeros(total.shape, F32)
    acc[...] = jnp.zeros(acc.shape, F32)
    dq[...] = jnp.zeros(dq.shape, F32)
    loads[0].wait()
    projected = dot(tok[...], wq[pl.ds(pl.multiple_of(t * WIDTH, WIDTH), WIDTH)], 1, 0)
    for load in loads[1:]:
        load.wait()
    for offset in (1, 3, 2):
        source = arrived(tok_all, offset, 0)
        rows = pl.ds(pl.multiple_of(source * WIDTH, WIDTH), WIDTH)
        if offset == 2:
            for copy in token_sends:
                copy.wait_send()
            sends.extend(spread(up, up_all, 1))
        projected = projected + dot(tok_all[source], wq[rows], 1, 0)

    c, s = cosine[...], sine[...]
    mine = pl.ds(pl.multiple_of(xh * ROWS, ROWS), ROWS)
    kv[0, z, mine] = turn(projected[:, 512:640], c, s).astype(BF16)
    kv[1, z, mine] = projected[:, 640:768].astype(BF16)
    x_kv = swap(kv.at[:, z, mine], kv.at[:, z, mine], 0)
    own_ring = gather_column(place, kv, xh, 0, ag_ss, ag_rs, sends)
    run(own_ring, 1)
    for h in range(QUERY_PER_KEY):
        q[pl.ds(h * ROWS, ROWS)] = turn(
            projected[:, h * HEAD_SIZE : (h + 1) * HEAD_SIZE], c, s
        ).astype(BF16)
    theirs = pl.ds(pl.multiple_of((1 - xh) * ROWS, ROWS), ROWS)
    other = kv.at[:, z, theirs]
    remote(other, other, x_ss.at[0], x_rs.at[0], place.xdev()).wait_recv()
    sends.append(x_kv)
    other_ring = gather_column(place, kv, 1 - xh, 1, ag_ss, ag_rs, sends)
    run(other_ring, 1)
    x_tok = [swap(tok_all.at[2 * (1 - xh)], tok_other.at[0], 1)]

    def around(step):
        return lax.rem(z + step + NZ, NZ)

    def forward(zk):
        keys = kv[0, zk]
        values = kv[1, zk]
        for cut in range(0, QROWS, HEAD_SIZE):
            cut = slice(cut, cut + HEAD_SIZE)
            scores = dot(keys, q[cut], 1, 1)
            allowed = key_place[...] <= limit[:, cut] - zk * ROWS
            scores = jnp.where(allowed, scores, -jnp.inf)
            before = top[:, cut]
            now = jnp.maximum(before, jnp.max(scores, axis=0, keepdims=True))
            weights = jnp.exp2((scores - now) * SCALE2)
            alpha = jnp.exp2((before - now) * SCALE2)
            top[:, cut] = now
            total[:, cut] = total[:, cut] * alpha + jnp.sum(weights, axis=0, keepdims=True)
            acc[:, cut] = acc[:, cut] * alpha + dot(values, weights.astype(BF16), 0, 0)

    def merged_term(source):
        columns = pl.ds(pl.multiple_of(source * WIDTH, WIDTH), WIDTH)
        return dot(up_all[source], wo[:, columns], 1, 1)

    def step_rings():
        run(own_ring, 1)
        run(other_ring, 1)

    forward(z)
    step_rings()
    forward(around(1))
    forward(around(-1))
    load_wo.wait()
    step_rings()
    forward(around(2))
    forward(around(-2))
    grad = merged_term(t)
    grad = grad + merged_term(arrived(up_all, 1, 1))
    step_rings()
    forward(around(3))
    forward(around(-3))
    grad = grad + merged_term(arrived(up_all, 3, 1))
    grad = grad + merged_term(arrived(up_all, 2, 1))
    x_up = [swap(up_all.at[2 * (1 - xh) + i], up_other.at[i], 2 + i) for i in range(2)]
    for h in range(QUERY_PER_KEY):
        do[pl.ds(h * ROWS, ROWS)] = grad[:, h * HEAD_SIZE : (h + 1) * HEAD_SIZE].astype(BF16)
    run(own_ring)
    run(other_ring)
    forward(around(4))

    out_t = (acc[...] / total[...]).astype(BF16)
    out = out_t.astype(F32).T.astype(BF16)
    for h in range(QUERY_PER_KEY):
        merged[:, h * HEAD_SIZE : (h + 1) * HEAD_SIZE] = out[h * ROWS : (h + 1) * ROWS]
    x_merged = swap(merged, merged_other, 4)
    logsum[...] = top[...] * SCALE2 + jnp.log2(total[...])
    delta[...] = jnp.sum(do[...].astype(F32).T * out_t.astype(F32), axis=0, keepdims=True)

    def backward(zk):
        keys = kv[0, zk]
        values = kv[1, zk]
        dk = jnp.zeros((PAIR, HEAD_SIZE), F32)
        dv = jnp.zeros((PAIR, HEAD_SIZE), F32)
        scores = dot(keys, q[...], 1, 1)
        allowed = key_place[:, 0:1] <= limit[...] - zk * ROWS
        probs = jnp.exp2(jnp.where(allowed, scores * SCALE2 - logsum[...], -jnp.inf))
        grad_probs = dot(values, do[...], 1, 1)
        grad_scores = (probs * (grad_probs - delta[...])).astype(BF16)
        dv = dot(probs.astype(BF16), do[...], 1, 0).astype(BF16)
        dk = (dot(grad_scores, q[...], 1, 0) * SCALE).astype(BF16)
        dq[...] += dot(keys, grad_scores, 0, 0)
        for column in range(2):
            rows = slice(column * ROWS, (column + 1) * ROWS)
            dkv[zk, column, 0:ROWS] = dk[rows]
            dkv[zk, column, ROWS:PAIR] = dv[rows]

    def load_kv(dest, sub, part):
        ref = dkv.at[dest, (1 - xh) if sub == 0 else xh]
        if part is not None:
            return ref[pl.ds(part * ROWS, ROWS)].astype(F32)
        return ref[...].astype(F32)

    def done_kv(sub, value):
        if sub == 0:
            kv_out[...] = value.astype(BF16)
        else:
            kv_own[...] = value

    ring_kv = scatter_ring(
        place, (0, 1), PAIR, load_kv, kv_sb, kv_rb, kv_ss, kv_rs, sends, done_kv
    )

    def attended_term(dest):
        return dot(merged[...], wo[:, pl.ds(pl.multiple_of(dest * WIDTH, WIDTH), WIDTH)], 1, 0)

    backward(around(4))
    run(ring_kv, 2)
    scatter_tensor(attended_term, att_own, att_s, att_r, 2)
    backward(around(3))
    backward(around(-3))
    run(ring_kv, 2)
    backward(around(2))
    backward(around(-2))
    run(ring_kv, 2)
    backward(around(1))
    backward(around(-1))
    run(ring_kv, 2)
    backward(z)

    def squeeze(value, column):
        e = expo[:, column : column + 1]
        sent = jnp.clip(value * jnp.exp2(-e), -127.0, 127.0).astype(BF16)
        return sent.astype(F32) * jnp.exp2(e)

    grad = dq[...].T * SCALE
    for h in range(QUERY_PER_KEY):
        gqkv[0, :, h * HEAD_SIZE : (h + 1) * HEAD_SIZE] = turn(
            squeeze(grad[h * ROWS : (h + 1) * ROWS], h), c, -s
        ).astype(BF16)
    x_gq = swap(gqkv.at[0, :, pl.ds(0, 512)], gqkv.at[1, :, pl.ds(0, 512)], 5)
    x_tok.append(swap(tok_all.at[2 * (1 - xh) + 1], tok_other.at[1], 6))
    run(ring_kv)
    x_dkv = swap(kv_out, kv_in, 7)

    def columns(dest):
        return pl.ds(pl.multiple_of(lax.rem(dest, 4) * 256, 256), 256)

    def load_o(dest, sub, part):
        first = sub * 256 + (0 if part is None else part * 128)
        last = first + (256 if part is None else 128)
        shard = lax.div(dest, 4)
        value = dot(merged[:, first:last], up_all[2 * xh + shard, :, columns(dest)], 0, 0)
        return value + dot(
            merged_other[:, first:last], up_other[shard, :, columns(dest)], 0, 0
        )

    def done_o(sub, value):
        gwo[pl.ds(sub * 256, 256)] = value.astype(BF16)

    def load_q(dest, sub, part):
        shard = lax.div(dest, 4)
        left = tok_all[2 * xh + shard, :, columns(dest)]
        left_other = tok_other[shard, :, columns(dest)]
        if part is not None:
            left = left[:, part * 128 : (part + 1) * 128]
            left_other = left_other[:, part * 128 : (part + 1) * 128]
        cut = slice(sub * 256, (sub + 1) * 256)
        return dot(left, gqkv[0, :, cut], 0, 0) + dot(left_other, gqkv[1, :, cut], 0, 0)

    def done_q(sub, value):
        gwq[:, sub * 256 : (sub + 1) * 256] = value.astype(BF16)

    ring_o = scatter_ring(place, (0, 1), 256, load_o, o_sb, o_rb, o_ss, o_rs, sends, done_o)
    ring_q = scatter_ring(place, (0, 1), 256, load_q, q_sb, q_rb, q_ss, q_rs, sends, done_q)
    ring_k = scatter_ring(place, (2,), 256, load_q, q_sb, q_rb, q_ss, q_rs, sends, done_q)
    for copy in x_up:
        copy.wait()
    x_merged.wait()
    run(ring_o, 4)
    x_dkv.wait()
    grad = kv_own[...] + kv_in[...]
    gqkv[0, :, 512:640] = turn(squeeze(grad[:ROWS], 4), c, -s).astype(BF16)
    gqkv[0, :, 640:768] = squeeze(grad[ROWS:], 5).astype(BF16)
    x_gkv = swap(gqkv.at[0, :, pl.ds(512, 256)], gqkv.at[1, :, pl.ds(512, 256)], 8)
    run(ring_o, 2)

    def tokens_term(dest):
        return dot(gqkv[0], wq[pl.ds(pl.multiple_of(dest * WIDTH, WIDTH), WIDTH)], 1, 1)

    scatter_tensor(tokens_term, tok_own, tok_s, tok_r, 3)
    run(ring_o, 2)
    x_gq.wait()
    for copy in x_tok:
        copy.wait()
    run(ring_q, 2)
    run(ring_o)
    collect_tensor(att_own, att_r, 2, attended)
    run(ring_q, 2)
    x_gkv.wait()
    run(ring_k, 1)
    run(ring_q, 2)
    run(ring_k, 1)
    collect_tensor(tok_own, tok_r, 3, grad_tokens)
    run(ring_q, 2)
    run(ring_k, 2)
    run(ring_q)
    run(ring_k)
    for copy in sends:
        copy.wait_send()


def layer(tok, up, wq, wo, freqs, exponents):
    vmem = pl.BlockSpec(memory_space=pltpu.VMEM)
    hbm = pl.BlockSpec(memory_space=pl.ANY)
    shape = jax.ShapeDtypeStruct
    dma = pltpu.SemaphoreType.DMA
    buf = pltpu.VMEM
    heads = QUERY_PER_KEY * HEAD_SIZE
    return pl.pallas_call(
        layer_kernel,
        name="layer",
        out_shape=[
            shape((ROWS, WIDTH), BF16),
            shape((ROWS, WIDTH), BF16),
            shape((256, 768), BF16),
            shape((512, 256), BF16),
        ],
        in_specs=[vmem, vmem, hbm, hbm, vmem, vmem],
        out_specs=[vmem] * 4,
        scratch_shapes=[
            buf(wq.shape, BF16),
            buf(wo.shape, BF16),
            buf((NT, ROWS, WIDTH), BF16),
            buf((NT, ROWS, WIDTH), BF16),
            buf((2, ROWS, WIDTH), BF16),
            buf((2, ROWS, WIDTH), BF16),
            buf((ROWS, HEAD_SIZE), F32),
            buf((ROWS, HEAD_SIZE), F32),
            buf((ROWS, 6), F32),
            buf((QROWS, HEAD_SIZE), BF16),
            buf((2, NZ, PAIR, HEAD_SIZE), BF16),
            buf((QROWS, HEAD_SIZE), BF16),
            buf((ROWS, heads), BF16),
            buf((ROWS, heads), BF16),
            buf((2, ROWS, 768), BF16),
            buf((PAIR, HEAD_SIZE), jnp.int32),
            buf((1, QROWS), jnp.int32),
            buf((1, QROWS), F32),
            buf((1, QROWS), F32),
            buf((HEAD_SIZE, QROWS), F32),
            buf((1, QROWS), F32),
            buf((1, QROWS), F32),
            buf((HEAD_SIZE, QROWS), F32),
            buf((NZ, 2, PAIR, HEAD_SIZE), BF16),
            buf((PAIR, HEAD_SIZE), F32),
            buf((PAIR, HEAD_SIZE), BF16),
            buf((PAIR, HEAD_SIZE), BF16),
            buf((ROWS, WIDTH), F32),
            buf((3, ROWS, WIDTH), BF16),
            buf((3, ROWS, WIDTH), BF16),
            buf((ROWS, WIDTH), F32),
            buf((3, ROWS, WIDTH), BF16),
            buf((3, ROWS, WIDTH), BF16),
            buf((2, 4, 2, PAIR, HEAD_SIZE), BF16),
            buf((2, 4, 2, PAIR, HEAD_SIZE), BF16),
            buf((2, 4, 2, 256, 256), BF16),
            buf((2, 4, 2, 256, 256), BF16),
            buf((2, 4, 3, 256, 256), BF16),
            buf((2, 4, 3, 256, 256), BF16),
            dma((5,)),
            dma((4, 3)),
            dma((4, 3)),
            dma((9,)),
            dma((9,)),
            dma((2, 2, 4)),
            dma((2, 2, 4)),
            dma((2, 4, 2)),
            dma((2, 4, 2)),
            dma((2, 4, 2)),
            dma((2, 4, 2)),
            dma((2, 4, 3)),
            dma((2, 4, 3)),
        ],
        compiler_params=pltpu.CompilerParams(
            collective_id=0, has_side_effects=True, vmem_limit_bytes=VMEM_LIMIT
        ),
    )(tok, up, wq, wo, freqs, exponents)


def settle_kernel(*refs):
    number = len(refs) // 2
    for i in range(number):
        refs[number + i][...] = refs[i][...]


def settle(*arrays):
    vmem = pl.BlockSpec(memory_space=pltpu.VMEM)
    return pl.pallas_call(
        settle_kernel,
        name="settle",
        out_shape=[jax.ShapeDtypeStruct(a.shape, a.dtype) for a in arrays],
        in_specs=[vmem] * len(arrays),
        out_specs=[vmem] * len(arrays),
        compiler_params=pltpu.CompilerParams(vmem_limit_bytes=VMEM_LIMIT),
    )(*arrays)


def local(tokens, input_projection_weight, w_out, upstream, exponents):
    half = HEAD_SIZE // 2
    freqs = jnp.power(F32(THETA), -jnp.arange(half, dtype=F32) * 2.0 / HEAD_SIZE)
    freqs = jnp.tile(freqs, 2).reshape(1, HEAD_SIZE)
    return settle(
        *layer(tokens, upstream, input_projection_weight, w_out, freqs, exponents)
    )


def solution(mesh):
    in_specs = (
        P(("dp", "seq"), "tensor"),
        P(None, "tensor"),
        P("tensor", None),
        P(("dp", "seq"), "tensor"),
        P("dp", "tensor"),
    )
    out_specs = (
        P(("dp", "seq"), "tensor"),
        P(("dp", "seq"), "tensor"),
        P(("dp", "seq"), "tensor"),
        P(("dp", "tensor"), "seq"),
    )
    return jax.shard_map(local, mesh=mesh, in_specs=in_specs, out_specs=out_specs, check_vma=False)
```

```python
import functools
import math

import jax
import jax.numpy as jnp
import numpy as np
from jax import lax
from jax.experimental import pallas as pl
from jax.experimental.pallas import tpu as pltpu
from jax.sharding import PartitionSpec as P

HEAD_SIZE = 128
QUERY_PER_KEY = 4
SCALE_TOKENS = 16
THETA = 500000.0

NZ = 8
NT = 4
ROWS = 192
QROWS = QUERY_PER_KEY * ROWS
PAIR = 2 * ROWS
WIDTH = 1024
MESH = pl.DeviceIdType.MESH
BF16 = jnp.bfloat16
F32 = jnp.float32
SCALE = 1.0 / math.sqrt(HEAD_SIZE)
SCALE2 = SCALE * math.log2(math.e)
VMEM_LIMIT = 60 * 2**20


def dot(left, right, left_dim, right_dim):
    return lax.dot_general(
        left, right, (((left_dim,), (right_dim,)), ((), ())), preferred_element_type=F32
    )


class Place:
    def __init__(self):
        self.d = lax.axis_index("dp")
        self.s = lax.axis_index("seq")
        self.t = lax.axis_index("tensor")
        self.xh = lax.div(self.s, NZ)
        self.z = lax.rem(self.s, NZ)

    def tensor(self, offset):
        return (self.d, self.s, lax.rem(self.t + offset, NT))

    def zdev(self, sign):
        return (self.d, self.xh * NZ + lax.rem(self.z + sign + NZ, NZ), self.t)

    def xdev(self):
        return (self.d, (1 - self.xh) * NZ + self.z, self.t)

    def diagonal(self, sign):
        return (self.d, (1 - self.xh) * NZ + lax.rem(self.z + sign + NZ, NZ), self.t)

    def enter(self):
        barrier = pltpu.get_barrier_semaphore()
        partners = [self.tensor(1), self.tensor(2), self.tensor(3)]
        partners += [self.zdev(1), self.zdev(-1), self.xdev()]
        partners += [self.diagonal(1), self.diagonal(-1)]
        for partner in partners:
            pl.semaphore_signal(barrier, inc=1, device_id=partner, device_id_type=MESH)
        pl.semaphore_wait(barrier, len(partners))


def remote(src, dst, send_sem, recv_sem, device):
    return pltpu.make_async_remote_copy(
        src_ref=src,
        dst_ref=dst,
        send_sem=send_sem,
        recv_sem=recv_sem,
        device_id=device,
        device_id_type=MESH,
    )


def turn(vectors, cosine, sine):
    return vectors * cosine + pltpu.roll(vectors, HEAD_SIZE // 2, 1) * sine


def gather_column(place, kv, cut, which, ss, rs, sends, first=1):
    def part(step, di, z):
        z = lax.rem(z + 2 * NZ, NZ)
        return kv.at[di, z, cut] if step == 4 else kv.at[:, z, cut]

    def arrived(step, di, sign):
        ref = part(step, di, place.z - sign * step)
        sem = rs.at[which, di, step - 1]
        remote(ref, ref, ss.at[which, di, step - 1], sem, place.zdev(sign)).wait_recv()

    for step in range(first, 5):
        for di, sign in ((0, 1), (1, -1)):
            if step > 1:
                arrived(step - 1, di, sign)
            ref = part(step, di, place.z - sign * (step - 1))
            copy = remote(
                ref,
                ref,
                ss.at[which, di, step - 1],
                rs.at[which, di, step - 1],
                place.zdev(sign),
            )
            copy.start()
            sends.append(copy)
        yield
    for di, sign in ((0, 1), (1, -1)):
        arrived(4, di, sign)


def scatter_ring(place, subs, rows, load, sbuf, rbuf, ss, rs, sends, done):
    half = rows // 2
    for step in (4, 3, 2, 1):
        for sub in subs:
            for di, sign in ((0, 1), (1, -1)):
                dest = lax.rem(place.z + sign * step + NZ, NZ)
                cut = pl.ds(di * half, half)
                here = sbuf.at[di, step - 1, sub]
                there = rbuf.at[di, step - 1, sub]
                if step == 4:
                    here, there = here.at[cut], there.at[cut]
                    here[...] = load(dest, sub, di, step, di).astype(BF16)
                else:
                    value = load(dest, sub, None, step, di)
                    before = rbuf.at[di, step, sub]
                    if step == 3:
                        before = before.at[cut]
                    remote(
                        before, before, ss.at[di, step, sub], rs.at[di, step, sub], place.zdev(sign)
                    ).wait_recv()
                    if step == 3:
                        here[cut] = (value[di * half : (di + 1) * half] + before[...]).astype(BF16)
                        rest = 1 - di
                        here[pl.ds(rest * half, half)] = value[
                            rest * half : (rest + 1) * half
                        ].astype(BF16)
                    else:
                        here[...] = (value + before[...]).astype(BF16)
                copy = remote(
                    here, there, ss.at[di, step - 1, sub], rs.at[di, step - 1, sub], place.zdev(sign)
                )
                copy.start()
                sends.append(copy)
            yield
    for sub in subs:
        total = load(place.z, sub, None, 0, 0)
        for di, sign in ((0, 1), (1, -1)):
            ref = rbuf.at[di, 0, sub]
            remote(ref, ref, ss.at[di, 0, sub], rs.at[di, 0, sub], place.zdev(sign)).wait_recv()
            total = total + ref[...]
        done(sub, total)


def run(steps, count=None):
    if count is None:
        for _ in steps:
            pass
    else:
        for _ in range(count):
            next(steps)


def layer_kernel(
    tok, up, wq_hbm, wo_hbm, freqs, exponents,
    attended_hbm, grad_tokens_hbm, gwq_hbm, gwo_hbm,
    wq, wo, tok_all, up_all, tok_other, up_other, cosine, sine, expo,
    q, kv, do, merged, merged_other, gqkv,
    key_place, limit, top, total, acc, logsum, delta, dq,
    dkv, dkv_other, kv_sum,
    att_own, att_s, att_r, tok_own, tok_s, tok_r,
    kv_sb, kv_rb, o_sb, o_rb, q_sb, q_rb,
    attended, grad_tokens, gwq, gwo,
    load_sem, store_sem, y_ss, y_rs, x_ss, x_rs, ag_ss, ag_rs,
    kv_ss, kv_rs, o_ss, o_rs, q_ss, q_rs,
):
    place = Place()
    t, xh, z = place.t, place.xh, place.z
    loads = []
    for i in range(NT):
        rows = pl.ds(pl.multiple_of(lax.rem(t + (0, 1, 3, 2)[i], NT) * WIDTH, WIDTH), WIDTH)
        loads.append(pltpu.make_async_copy(wq_hbm.at[rows], wq.at[rows], load_sem.at[i]))
        loads[-1].start()
    load_wo = pltpu.make_async_copy(wo_hbm, wo, load_sem.at[4])
    load_wo.start()
    place.enter()
    sends = []

    def swap(src, dst, i):
        copy = remote(src, dst, x_ss.at[i], x_rs.at[i], place.xdev())
        copy.start()
        return copy

    def on_y(src, dst, which, i, offset):
        return remote(src, dst, y_ss.at[which, i], y_rs.at[which, i], place.tensor(offset))

    before, after, across = (lax.rem(t + i, NT) for i in (3, 1, 2))

    def halves(first, rows):
        return pl.ds(first, rows // 2), pl.ds(first + rows // 2, rows // 2)

    def tensor_start(own, everyone, which, first=0, rows=ROWS):
        part = pl.ds(first, rows)
        for i, offset in ((0, 1), (1, 3)):
            copy = on_y(own.at[part], everyone.at[t, part], which, i, offset)
            copy.start()
            sends.append(copy)

    def tensor_forward(everyone, which, first=0, rows=ROWS):
        for i, offset, source in ((0, 1, before), (1, 3, after)):
            ref = everyone.at[source, pl.ds(first, rows)]
            on_y(ref, ref, which, i, offset).wait_recv()
            ref = everyone.at[source, halves(first, rows)[i]]
            copy = on_y(ref, ref, which, 2 + i, offset)
            copy.start()
            sends.append(copy)

    def tensor_end(everyone, which, first=0, rows=ROWS):
        for i, offset in ((0, 1), (1, 3)):
            ref = everyone.at[across, halves(first, rows)[i]]
            on_y(ref, ref, which, 2 + i, offset).wait_recv()

    gives = lax.div(t, 2) == 1 - xh
    holds = lax.div(t, 2) == xh
    slot = lax.rem(t, 2)

    def give(own, others, i):
        @pl.when(gives)
        def _():
            remote(own, others.at[slot], x_ss.at[i], x_rs.at[i], place.xdev()).start()

    def holder(source):
        return lax.div(source, 2) == xh

    def share_start(own, others, i, which):
        @pl.when(holds)
        def _():
            ref = others.at[slot]
            remote(own, ref, x_ss.at[i], x_rs.at[i], place.xdev()).wait_recv()
            on_y(ref, ref, which, 0, 1).start()
            on_y(ref, ref, which, 1, 3).start()

    def share_forward(others, which):
        for i, offset, source in ((0, 1, before), (1, 3, after)):

            @pl.when(holder(source))
            def _(i=i, offset=offset, source=source):
                ref = others.at[lax.rem(source, 2)]
                on_y(ref, ref, which, i, offset).wait_recv()
                ref = others.at[lax.rem(source, 2), halves(0, ROWS)[i]]
                on_y(ref, ref, which, 2 + i, offset).start()

    def share_end(others, which):
        @pl.when(holder(across))
        def _():
            for i, offset in ((0, 1), (1, 3)):
                ref = others.at[lax.rem(across, 2), halves(0, ROWS)[i]]
                on_y(ref, ref, which, 2 + i, offset).wait_recv()

    def share_sent(own, others, i, which):
        @pl.when(gives)
        def _():
            remote(own, others.at[slot], x_ss.at[i], x_rs.at[i], place.xdev()).wait_send()

        @pl.when(holds)
        def _():
            ref = others.at[slot]
            on_y(ref, ref, which, 0, 1).wait_send()
            on_y(ref, ref, which, 1, 3).wait_send()

        for i, offset, source in ((0, 1, before), (1, 3, after)):

            @pl.when(holder(source))
            def _(i=i, offset=offset, source=source):
                ref = others.at[lax.rem(source, 2), halves(0, ROWS)[i]]
                on_y(ref, ref, which, 2 + i, offset).wait_send()

    stores = []

    def store(src, dst):
        copy = pltpu.make_async_copy(src, dst, store_sem.at[len(stores)])
        copy.start()
        stores.append(copy)

    def scatter_tensor(term, own, sbuf, rbuf, which):
        for offset in (1, 3, 2):
            sbuf[offset - 1] = term(lax.rem(t + offset, NT)).astype(BF16)
            copy = remote(
                sbuf.at[offset - 1],
                rbuf.at[offset - 1],
                y_ss.at[which, offset - 1],
                y_rs.at[which, offset - 1],
                place.tensor(offset),
            )
            copy.start()
            sends.append(copy)
        own[...] = term(t)

    def collect_tensor(own, rbuf, which, out):
        value = own[...]
        for offset in (1, 3, 2):
            ref = rbuf.at[offset - 1]
            remote(
                ref,
                ref,
                y_ss.at[which, offset - 1],
                y_rs.at[which, offset - 1],
                place.tensor(offset),
            ).wait_recv()
            value = value + ref[...]
        out[...] = value.astype(BF16)

    half = ROWS // 2
    tensor_start(tok, tok_all, 0, 0, half)
    give(up, up_other, 2)
    tok_all[t] = tok[...]
    up_all[t] = up[...]
    position = lax.broadcasted_iota(jnp.int32, (ROWS, HEAD_SIZE), 0) + place.s * ROWS
    angles = position.astype(F32) * freqs[...]
    cosine[...] = jnp.cos(angles)
    low = lax.broadcasted_iota(jnp.int32, (ROWS, HEAD_SIZE), 1) < HEAD_SIZE // 2
    sines = jnp.sin(angles)
    sine[...] = jnp.where(low, -sines, sines)
    groups = exponents.shape[1]
    group = lax.broadcasted_iota(jnp.int32, (ROWS, groups), 0) // SCALE_TOKENS
    group = group + place.s * (ROWS // SCALE_TOKENS)
    pick = lax.broadcasted_iota(jnp.int32, (ROWS, groups), 1) == group
    expo[...] = dot(pick.astype(F32).astype(BF16), exponents[...].astype(F32).astype(BF16), 1, 1)
    row = lax.broadcasted_iota(jnp.int32, (PAIR, HEAD_SIZE), 0)
    key_place[...] = jnp.where(row < ROWS, row, row + (NZ - 1) * ROWS)
    limit[...] = place.s * ROWS + lax.rem(
        lax.broadcasted_iota(jnp.int32, (1, QROWS), 1), jnp.int32(ROWS)
    )
    top[...] = jnp.full(top.shape, -jnp.inf, F32)
    total[...] = jnp.zeros(total.shape, F32)
    acc[...] = jnp.zeros(acc.shape, F32)
    dq[...] = jnp.zeros(dq.shape, F32)
    def weight_rows(source):
        return pl.ds(pl.multiple_of(source * WIDTH, WIDTH), WIDTH)

    def project_kv(first, sources):
        part = pl.ds(first, half)
        return sum(
            dot(tok_all[source, part], wq[weight_rows(source), 512:768], 1, 0)
            for source in sources
        )

    def project_q(source):
        return dot(tok_all[source], wq[weight_rows(source), 0:512], 1, 0)

    def around(step):
        return lax.rem(z + step + NZ, NZ)

    def forward(zk):
        keys = kv[0, zk]
        values = kv[1, zk]
        for cut in range(0, QROWS, HEAD_SIZE):
            cut = slice(cut, cut + HEAD_SIZE)
            scores = dot(keys, q[cut], 1, 1)
            allowed = key_place[...] <= limit[:, cut] - zk * ROWS
            scores = jnp.where(allowed, scores, -jnp.inf)
            before = top[:, cut]
            now = jnp.maximum(before, jnp.max(scores, axis=0, keepdims=True))
            weights = jnp.exp2((scores - now) * SCALE2)
            alpha = jnp.exp2((before - now) * SCALE2)
            top[:, cut] = now
            total[:, cut] = total[:, cut] * alpha + jnp.sum(weights, axis=0, keepdims=True)
            acc[:, cut] = acc[:, cut] * alpha + dot(values, weights.astype(BF16), 0, 0)

    def merged_term(source):
        return dot(up_all[source], wo[:, weight_rows(source)], 1, 1)

    c, s = cosine[...], sine[...]
    own_rings, other_rings, x_kv = [], [], []

    def column_part(column, first):
        return pl.ds(pl.multiple_of(column * ROWS + first, half), half)

    def send_kv(i, projected):
        first = i * half
        part = slice(first, first + half)
        rows = column_part(xh, first)
        kv[0, z, rows] = turn(projected[:, 0:128], c[part], s[part]).astype(BF16)
        kv[1, z, rows] = projected[:, 128:256].astype(BF16)
        x_kv.append(swap(kv.at[:, z, rows], kv.at[:, z, rows], (0, 14)[i]))
        own_rings.append(gather_column(place, kv, rows, i, ag_ss, ag_rs, sends))
        run(own_rings[i], 1)
        for di, sign in ((0, 1), (1, -1)):
            ref = kv.at[:, z, rows]
            copy = remote(
                ref, ref, ag_ss.at[2 + i, di, 0], ag_rs.at[2 + i, di, 0], place.diagonal(sign)
            )
            copy.start()
            sends.append(copy)
        other = column_part(1 - xh, first)
        other_rings.append(gather_column(place, kv, other, 2 + i, ag_ss, ag_rs, sends, 2))

    def receive_kv(i):
        rows = column_part(1 - xh, i * half)
        ref = kv.at[:, z, rows]
        sem = (0, 14)[i]
        remote(ref, ref, x_ss.at[sem], x_rs.at[sem], place.xdev()).wait_recv()
        sends.append(x_kv[i])

    for load in loads:
        load.wait()
    tensor_forward(tok_all, 0, 0, half)
    tensor_start(tok, tok_all, 6, half, half)
    projected = project_kv(0, (t, before, after))
    tensor_end(tok_all, 0, 0, half)
    send_kv(0, projected + project_kv(0, (across,)))
    tensor_forward(tok_all, 6, half, half)
    projected = project_kv(half, (t, before, after))
    run(own_rings[0], 1)
    run(other_rings[0], 1)
    tensor_end(tok_all, 6, half, half)
    tensor_start(up, up_all, 1)
    send_kv(1, projected + project_kv(half, (across,)))
    run(own_rings[0], 1)
    run(other_rings[0], 1)
    projected = project_q(t) + project_q(before) + project_q(after) + project_q(across)
    for h in range(QUERY_PER_KEY):
        q[pl.ds(h * ROWS, ROWS)] = turn(
            projected[:, h * HEAD_SIZE : (h + 1) * HEAD_SIZE], c, s
        ).astype(BF16)
    share_start(up, up_other, 2, 2)
    run(own_rings[1], 1)
    run(other_rings[1], 1)
    receive_kv(0)
    receive_kv(1)
    give(tok, tok_other, 1)
    forward(z)
    run(own_rings[0], 1)
    run(other_rings[0], 1)
    run(own_rings[1], 1)
    run(other_rings[1], 1)
    run(own_rings[0])
    run(other_rings[0])
    forward(around(1))
    forward(around(-1))
    run(own_rings[1], 1)
    run(other_rings[1], 1)
    forward(around(2))
    forward(around(-2))
    tensor_forward(up_all, 1)
    load_wo.wait()
    forward(around(3))
    forward(around(-3))
    share_forward(up_other, 2)
    run(own_rings[1])
    run(other_rings[1])
    forward(around(4))

    out_t = (acc[...] / total[...]).astype(BF16)
    out = out_t.astype(F32).T.astype(BF16)
    for h in range(QUERY_PER_KEY):
        merged[:, h * HEAD_SIZE : (h + 1) * HEAD_SIZE] = out[h * ROWS : (h + 1) * ROWS]
    x_merged = []
    for i, sem in enumerate((3, 15)):
        ref = pl.ds(i * 256, 256)
        x_merged.append(swap(merged.at[:, ref], merged_other.at[:, ref], sem))
    tensor_end(up_all, 1)
    grad = merged_term(t) + merged_term(before) + merged_term(after) + merged_term(across)
    for h in range(QUERY_PER_KEY):
        do[pl.ds(h * ROWS, ROWS)] = grad[:, h * HEAD_SIZE : (h + 1) * HEAD_SIZE].astype(BF16)
    logsum[...] = top[...] * SCALE2 + jnp.log2(total[...])
    delta[...] = jnp.sum(do[...].astype(F32).T * out_t.astype(F32), axis=0, keepdims=True)

    def backward(slot, zk):
        keys = kv[0, zk]
        values = kv[1, zk]
        scores = dot(keys, q[...], 1, 1)
        allowed = key_place[:, 0:1] <= limit[...] - zk * ROWS
        probs = jnp.exp2(jnp.where(allowed, scores * SCALE2 - logsum[...], -jnp.inf))
        grad_probs = dot(values, do[...], 1, 1)
        grad_scores = (probs * (grad_probs - delta[...])).astype(BF16)
        dv = dot(probs.astype(BF16), do[...], 1, 0).astype(BF16)
        dk = (dot(grad_scores, q[...], 1, 0) * SCALE).astype(BF16)
        dq[...] += dot(keys, grad_scores, 0, 0)
        for column in range(2):
            rows = slice(column * ROWS, (column + 1) * ROWS)
            dkv[slot, column, 0:ROWS] = dk[rows]
            dkv[slot, column, ROWS:PAIR] = dv[rows]
        sends.append(swap(dkv.at[slot, 1 - xh], dkv_other.at[slot], 6 + slot))

    kv_here = set()

    def load_kv(dest, sub, part, step, di):
        slot = {4: 0, 3: 1, 2: 3, 1: 5, 0: 7}[step] + (di if step in (1, 2, 3) else 0)
        ref = dkv_other.at[slot]
        if slot not in kv_here:
            kv_here.add(slot)
            remote(ref, ref, x_ss.at[6 + slot], x_rs.at[6 + slot], place.xdev()).wait_recv()
        rows = pl.ds(sub * ROWS, ROWS)
        if part is not None:
            rows = pl.ds(sub * ROWS + part * (ROWS // 2), ROWS // 2)
        return dkv[slot, xh, rows].astype(F32) + ref[rows].astype(F32)

    def done_kv(sub, value):
        kv_sum[pl.ds(sub * ROWS, ROWS)] = value

    ring_kv = scatter_ring(
        place, (0, 1), ROWS, load_kv, kv_sb, kv_rb, kv_ss, kv_rs, sends, done_kv
    )

    def attended_term(dest):
        return dot(merged[...], wo[:, pl.ds(pl.multiple_of(dest * WIDTH, WIDTH), WIDTH)], 1, 0)

    def columns(dest):
        return pl.ds(pl.multiple_of(lax.rem(dest, 4) * 256, 256), 256)

    def load_o(dest, sub, part, step, di):
        first = sub * 256 + (0 if part is None else part * 128)
        last = first + (256 if part is None else 128)
        shard = lax.div(dest, 4)
        value = dot(merged[:, first:last], up_all[2 * xh + shard, :, columns(dest)], 0, 0)
        return value + dot(
            merged_other[:, first:last], up_other[shard, :, columns(dest)], 0, 0
        )

    def done_o(sub, value):
        gwo[pl.ds(sub * 256, 256)] = value.astype(BF16)

    def load_q(dest, sub, part, step, di):
        shard = lax.div(dest, 4)
        left = tok_all[2 * xh + shard, :, columns(dest)]
        left_other = tok_other[shard, :, columns(dest)]
        if part is not None:
            left = left[:, part * 128 : (part + 1) * 128]
            left_other = left_other[:, part * 128 : (part + 1) * 128]
        cut = slice(sub * 256, (sub + 1) * 256)
        return dot(left, gqkv[0, :, cut], 0, 0) + dot(left_other, gqkv[1, :, cut], 0, 0)

    def done_q(sub, value):
        cut = pl.ds(sub * 256, 256)
        gwq[sub] = value.astype(BF16)
        store(gwq.at[sub], gwq_hbm.at[:, cut])

    ring_o = scatter_ring(place, (0, 1), 256, load_o, o_sb, o_rb, o_ss, o_rs, sends, done_o)
    ring_q = scatter_ring(place, (0, 1), 256, load_q, q_sb, q_rb, q_ss, q_rs, sends, done_q)
    ring_k = scatter_ring(place, (2,), 256, load_q, q_sb, q_rb, q_ss, q_rs, sends, done_q)

    def squeeze(value, column):
        e = expo[:, column : column + 1]
        sent = jnp.clip(value * jnp.exp2(-e), -127.0, 127.0).astype(BF16)
        return sent.astype(F32) * jnp.exp2(e)

    share_start(tok, tok_other, 1, 3)
    backward(0, around(4))
    backward(1, around(3))
    backward(2, around(-3))
    x_merged[0].wait()
    share_end(up_other, 2)
    run(ring_o, 1)
    x_merged[1].wait()
    run(ring_o, 1)
    backward(3, around(2))
    backward(4, around(-2))
    run(ring_kv, 2)
    run(ring_o, 2)
    share_forward(tok_other, 3)
    backward(5, around(1))
    backward(6, around(-1))
    backward(7, z)
    run(ring_kv, 2)
    grad = dq[...].T * SCALE
    for h in range(QUERY_PER_KEY):
        gqkv[0, :, h * HEAD_SIZE : (h + 1) * HEAD_SIZE] = turn(
            squeeze(grad[h * ROWS : (h + 1) * ROWS], h), c, -s
        ).astype(BF16)
    x_gq = swap(gqkv.at[0, :, pl.ds(0, 512)], gqkv.at[1, :, pl.ds(0, 512)], 4)
    run(ring_o, 2)
    scatter_tensor(attended_term, att_own, att_s, att_r, 4)
    run(ring_kv, 2)
    run(ring_o, 2)
    run(ring_kv, 2)
    x_gq.wait()
    share_end(tok_other, 3)
    run(ring_q, 2)
    run(ring_kv)
    gqkv[0, :, 512:640] = turn(squeeze(kv_sum[0:ROWS], 4), c, -s).astype(BF16)
    gqkv[0, :, 640:768] = squeeze(kv_sum[ROWS:PAIR], 5).astype(BF16)
    x_gkv = swap(gqkv.at[0, :, pl.ds(512, 256)], gqkv.at[1, :, pl.ds(512, 256)], 5)
    run(ring_o)
    store(gwo, gwo_hbm)
    run(ring_q, 2)

    def tokens_term(dest):
        return dot(gqkv[0], wq[pl.ds(pl.multiple_of(dest * WIDTH, WIDTH), WIDTH)], 1, 1)

    x_gkv.wait()
    run(ring_k, 1)
    scatter_tensor(tokens_term, tok_own, tok_s, tok_r, 5)
    run(ring_k, 1)
    run(ring_q, 2)
    run(ring_k, 1)
    collect_tensor(att_own, att_r, 4, attended)
    store(attended, attended_hbm)
    run(ring_q, 2)
    run(ring_k, 1)
    collect_tensor(tok_own, tok_r, 5, grad_tokens)
    store(grad_tokens, grad_tokens_hbm)
    run(ring_q)
    run(ring_k)
    share_sent(up, up_other, 2, 2)
    share_sent(tok, tok_other, 1, 3)
    for copy in sends:
        copy.wait_send()
    for copy in stores:
        copy.wait()


def layer(tok, up, wq, wo, freqs, exponents):
    vmem = pl.BlockSpec(memory_space=pltpu.VMEM)
    hbm = pl.BlockSpec(memory_space=pl.ANY)
    shape = jax.ShapeDtypeStruct
    dma = pltpu.SemaphoreType.DMA
    buf = pltpu.VMEM
    heads = QUERY_PER_KEY * HEAD_SIZE
    return pl.pallas_call(
        layer_kernel,
        name="layer",
        out_shape=[
            shape((ROWS, WIDTH), BF16),
            shape((ROWS, WIDTH), BF16),
            shape((256, 768), BF16),
            shape((512, 256), BF16),
        ],
        in_specs=[vmem, vmem, hbm, hbm, vmem, vmem],
        out_specs=[hbm] * 4,
        scratch_shapes=[
            buf(wq.shape, BF16),
            buf(wo.shape, BF16),
            buf((NT, ROWS, WIDTH), BF16),
            buf((NT, ROWS, WIDTH), BF16),
            buf((2, ROWS, WIDTH), BF16),
            buf((2, ROWS, WIDTH), BF16),
            buf((ROWS, HEAD_SIZE), F32),
            buf((ROWS, HEAD_SIZE), F32),
            buf((ROWS, 6), F32),
            buf((QROWS, HEAD_SIZE), BF16),
            buf((2, NZ, PAIR, HEAD_SIZE), BF16),
            buf((QROWS, HEAD_SIZE), BF16),
            buf((ROWS, heads), BF16),
            buf((ROWS, heads), BF16),
            buf((2, ROWS, 768), BF16),
            buf((PAIR, HEAD_SIZE), jnp.int32),
            buf((1, QROWS), jnp.int32),
            buf((1, QROWS), F32),
            buf((1, QROWS), F32),
            buf((HEAD_SIZE, QROWS), F32),
            buf((1, QROWS), F32),
            buf((1, QROWS), F32),
            buf((HEAD_SIZE, QROWS), F32),
            buf((NZ, 2, PAIR, HEAD_SIZE), BF16),
            buf((NZ, PAIR, HEAD_SIZE), BF16),
            buf((PAIR, HEAD_SIZE), F32),
            buf((ROWS, WIDTH), F32),
            buf((3, ROWS, WIDTH), BF16),
            buf((3, ROWS, WIDTH), BF16),
            buf((ROWS, WIDTH), F32),
            buf((3, ROWS, WIDTH), BF16),
            buf((3, ROWS, WIDTH), BF16),
            buf((2, 4, 2, ROWS, HEAD_SIZE), BF16),
            buf((2, 4, 2, ROWS, HEAD_SIZE), BF16),
            buf((2, 4, 2, 256, 256), BF16),
            buf((2, 4, 2, 256, 256), BF16),
            buf((2, 4, 3, 256, 256), BF16),
            buf((2, 4, 3, 256, 256), BF16),
            buf((ROWS, WIDTH), BF16),
            buf((ROWS, WIDTH), BF16),
            buf((3, 256, 256), BF16),
            buf((512, 256), BF16),
            dma((5,)),
            dma((6,)),
            dma((7, 4)),
            dma((7, 4)),
            dma((16,)),
            dma((16,)),
            dma((4, 2, 4)),
            dma((4, 2, 4)),
            dma((2, 4, 2)),
            dma((2, 4, 2)),
            dma((2, 4, 2)),
            dma((2, 4, 2)),
            dma((2, 4, 3)),
            dma((2, 4, 3)),
        ],
        compiler_params=pltpu.CompilerParams(
            collective_id=0, has_side_effects=True, vmem_limit_bytes=VMEM_LIMIT
        ),
    )(tok, up, wq, wo, freqs, exponents)


def settle_kernel(*refs):
    number = len(refs) // 2
    for i in range(number):
        refs[number + i][...] = refs[i][...]


def settle(*arrays):
    vmem = pl.BlockSpec(memory_space=pltpu.VMEM)
    return pl.pallas_call(
        settle_kernel,
        name="settle",
        out_shape=[jax.ShapeDtypeStruct(a.shape, a.dtype) for a in arrays],
        in_specs=[vmem] * len(arrays),
        out_specs=[vmem] * len(arrays),
        compiler_params=pltpu.CompilerParams(vmem_limit_bytes=VMEM_LIMIT),
    )(*arrays)


def local(tokens, input_projection_weight, w_out, upstream, exponents):
    half = HEAD_SIZE // 2
    freqs = np.power(np.float32(THETA), -np.arange(half, dtype=np.float32) * 2.0 / HEAD_SIZE)
    freqs = jnp.asarray(np.tile(freqs, 2).reshape(1, HEAD_SIZE), F32)
    return settle(
        *layer(tokens, upstream, input_projection_weight, w_out, freqs, exponents.T)
    )


def solution(mesh):
    in_specs = (
        P(("dp", "seq"), "tensor"),
        P(None, "tensor"),
        P("tensor", None),
        P(("dp", "seq"), "tensor"),
        P("dp", "tensor"),
    )
    out_specs = (
        P(("dp", "seq"), "tensor"),
        P(("dp", "seq"), "tensor"),
        P(("dp", "seq"), "tensor"),
        P(("dp", "tensor"), "seq"),
    )
    return jax.shard_map(local, mesh=mesh, in_specs=in_specs, out_specs=out_specs, check_vma=False)
```

```python
import functools
import math

import jax
import jax.numpy as jnp
import numpy as np
from jax import lax
from jax.experimental import pallas as pl
from jax.experimental.pallas import tpu as pltpu
from jax.sharding import PartitionSpec as P

HEAD_SIZE = 128
QUERY_PER_KEY = 4
SCALE_TOKENS = 16
THETA = 500000.0

NZ = 8
NT = 4
ROWS = 192
QROWS = QUERY_PER_KEY * ROWS
PAIR = 2 * ROWS
WIDTH = 1024
MESH = pl.DeviceIdType.MESH
BF16 = jnp.bfloat16
F32 = jnp.float32
SCALE = 1.0 / math.sqrt(HEAD_SIZE)
SCALE2 = SCALE * math.log2(math.e)
VMEM_LIMIT = 60 * 2**20


def dot(left, right, left_dim, right_dim):
    return lax.dot_general(
        left, right, (((left_dim,), (right_dim,)), ((), ())), preferred_element_type=F32
    )


class Place:
    def __init__(self):
        self.d = lax.axis_index("dp")
        self.s = lax.axis_index("seq")
        self.t = lax.axis_index("tensor")
        self.xh = lax.div(self.s, NZ)
        self.z = lax.rem(self.s, NZ)

    def tensor(self, offset):
        return (self.d, self.s, lax.rem(self.t + offset, NT))

    def zdev(self, sign):
        return (self.d, self.xh * NZ + lax.rem(self.z + sign + NZ, NZ), self.t)

    def xdev(self):
        return (self.d, (1 - self.xh) * NZ + self.z, self.t)

    def diagonal(self, sign):
        return (self.d, (1 - self.xh) * NZ + lax.rem(self.z + sign + NZ, NZ), self.t)

    def enter(self):
        barrier = pltpu.get_barrier_semaphore()
        partners = [self.tensor(1), self.tensor(2), self.tensor(3)]
        partners += [self.zdev(i) for i in range(1, NZ)] + [self.xdev()]
        partners += [self.diagonal(1), self.diagonal(-1)]
        for partner in partners:
            pl.semaphore_signal(barrier, inc=1, device_id=partner, device_id_type=MESH)
        pl.semaphore_wait(barrier, len(partners))


def remote(src, dst, send_sem, recv_sem, device):
    return pltpu.make_async_remote_copy(
        src_ref=src,
        dst_ref=dst,
        send_sem=send_sem,
        recv_sem=recv_sem,
        device_id=device,
        device_id_type=MESH,
    )


def turn(vectors, cosine, sine):
    return vectors * cosine + pltpu.roll(vectors, HEAD_SIZE // 2, 1) * sine


def gather_ring(place, part, which, ss, rs, sends, first=1):
    def arrived(step, di, sign):
        ref = part(step, di, place.z - sign * step)
        sem = rs.at[which, di, step - 1]
        remote(ref, ref, ss.at[0], sem, place.zdev(sign)).wait_recv()

    for step in range(first, 5):
        for di, sign in ((0, 1), (1, -1)):
            if step > 1:
                arrived(step - 1, di, sign)
            ref = part(step, di, place.z - sign * (step - 1))
            copy = remote(
                ref,
                ref,
                ss.at[0],
                rs.at[which, di, step - 1],
                place.zdev(sign),
            )
            copy.start()
            sends.append(copy)
        yield
    for di, sign in ((0, 1), (1, -1)):
        arrived(4, di, sign)


def scatter_ring(place, subs, rows, load, sbuf, rbuf, ss, rs, sends, done):
    half = rows // 2
    for step in (4, 3, 2, 1):
        for sub in subs:
            for di, sign in ((0, 1), (1, -1)):
                dest = lax.rem(place.z + sign * step + NZ, NZ)
                cut = pl.ds(di * half, half)
                here = sbuf.at[di, step - 1, sub]
                there = rbuf.at[di, step - 1, sub]
                if step == 4:
                    here, there = here.at[cut], there.at[cut]
                    here[...] = load(dest, sub, di, step, di).astype(BF16)
                else:
                    value = load(dest, sub, None, step, di)
                    before = rbuf.at[di, step, sub]
                    if step == 3:
                        before = before.at[cut]
                    remote(
                        before, before, ss.at[0], rs.at[di, step, sub], place.zdev(sign)
                    ).wait_recv()
                    if step == 3:
                        here[cut] = (value[di * half : (di + 1) * half] + before[...]).astype(BF16)
                        rest = 1 - di
                        here[pl.ds(rest * half, half)] = value[
                            rest * half : (rest + 1) * half
                        ].astype(BF16)
                    else:
                        here[...] = (value + before[...]).astype(BF16)
                copy = remote(
                    here, there, ss.at[0], rs.at[di, step - 1, sub], place.zdev(sign)
                )
                copy.start()
                sends.append(copy)
            yield
    for sub in subs:
        total = load(place.z, sub, None, 0, 0)
        for di, sign in ((0, 1), (1, -1)):
            ref = rbuf.at[di, 0, sub]
            remote(ref, ref, ss.at[0], rs.at[di, 0, sub], place.zdev(sign)).wait_recv()
            total = total + ref[...]
        done(sub, total)


def run(steps, count=None):
    if count is None:
        for _ in steps:
            pass
    else:
        for _ in range(count):
            next(steps)


class TwoStages:
    def __init__(self, place, rows, term, sbuf, rbuf, ss, rs, sends):
        self.place, self.half, self.term, self.sends = place, rows // 2, term, sends
        self.refs = sbuf, rbuf, ss, rs

    def copy(self, di, step, hops):
        sbuf, rbuf, ss, rs = self.refs
        at = (di, step - 1)
        here, there = sbuf.at[at], rbuf.at[at]
        if step == 4:
            cut = pl.ds(di * self.half, self.half)
            here, there = here.at[cut], there.at[cut]
        return remote(here, there, ss.at[0], rs.at[at], self.place.zdev(hops))

    def send(self, di, step, hops, value):
        sbuf = self.refs[0]
        if step == 4:
            cut = slice(di * self.half, (di + 1) * self.half)
            sbuf[di, step - 1, cut] = value[cut].astype(BF16)
        else:
            sbuf[di, step - 1] = value.astype(BF16)
        copy = self.copy(di, step, hops)
        copy.start()
        self.sends.append(copy)

    def far(self):
        value = self.term(4, 0)
        for di, sign in ((0, 1), (1, -1)):
            self.send(di, 3, sign, self.term(3, di))
            self.send(di, 4, 2 * sign, value)

    def near(self):
        for di, sign in ((0, 1), (1, -1)):
            self.send(di, 1, sign, self.term(1, di))

    def middle(self):
        half, (_, rbuf, _, _) = self.half, self.refs
        for di, sign in ((0, 1), (1, -1)):
            value = self.term(2, di)
            self.copy(di, 3, sign).wait_recv()
            self.copy(di, 4, 2 * sign).wait_recv()
            value = value + rbuf[di, 2]
            parts = [value[:half], value[half:]]
            parts[di] = parts[di] + rbuf[di, 3, di * half : (di + 1) * half]
            self.send(di, 2, 2 * sign, jnp.concatenate(parts, axis=0))

    def end(self):
        value = self.term(0, 0)
        for di, sign in ((0, 1), (1, -1)):
            for step in (1, 2):
                self.copy(di, step, step * sign).wait_recv()
                value = value + self.refs[1][di, step - 1]
        return value


def layer_kernel(
    tok_hbm, up_hbm, wq_hbm, wo_hbm, freqs, exponents,
    attended_hbm, grad_tokens_hbm, gwq_hbm, gwo_hbm,
    wq, wo, tok_all, up_all, tok_other, slab, cosine, sine, expo,
    q, kv, do, merged, merged_all, gqkv,
    key_place, limit, top, total, acc, logsum, delta, dq,
    dkv, dkv_other,
    att_own, att_s, att_r, tok_own, tok_s, tok_r,
    kv_sb, kv_rb, o_sb, o_rb, q_sb, q_rb, k_sb, k_rb,
    attended, grad_tokens, gwq, gwo,
    load_sem, store_sem, send_sem, y_rs, x_rs, ag_rs,
    kv_rs, m_rs, a_rs, q_rs, k_rs,
):
    place = Place()
    t, xh, z = place.t, place.xh, place.z
    tok, up = tok_all.at[t], up_all.at[t]
    load_tok = pltpu.make_async_copy(tok_hbm, tok, load_sem.at[5])
    load_tok.start()
    load_up = pltpu.make_async_copy(up_hbm, up, load_sem.at[6])
    load_up.start()
    loads = []
    for i in range(NT):
        rows = pl.ds(pl.multiple_of(lax.rem(t + (0, 1, 3, 2)[i], NT) * WIDTH, WIDTH), WIDTH)
        loads.append(pltpu.make_async_copy(wq_hbm.at[rows], wq.at[rows], load_sem.at[i]))
        loads[-1].start()
    load_wo = pltpu.make_async_copy(wo_hbm, wo, load_sem.at[4])
    load_wo.start()
    place.enter()
    sends = []
    half = ROWS // 2

    def swap(src, dst, i):
        copy = remote(src, dst, send_sem.at[0], x_rs.at[i], place.xdev())
        copy.start()
        sends.append(copy)
        return copy

    def on_y(src, dst, which, i, offset):
        return remote(src, dst, send_sem.at[0], y_rs.at[which, i], place.tensor(offset))

    before, after, across = (lax.rem(t + i, NT) for i in (3, 1, 2))

    def halves(first, rows):
        return pl.ds(first, rows // 2), pl.ds(first + rows // 2, rows // 2)

    def tensor_start(own, everyone, which, first=0, rows=ROWS):
        part = pl.ds(first, rows)
        for i, offset in ((0, 1), (1, 3)):
            copy = on_y(own.at[part], everyone.at[t, part], which, i, offset)
            copy.start()
            sends.append(copy)

    def tensor_forward(everyone, which, first=0, rows=ROWS):
        for i, offset, source in ((0, 1, before), (1, 3, after)):
            ref = everyone.at[source, pl.ds(first, rows)]
            on_y(ref, ref, which, i, offset).wait_recv()
            ref = everyone.at[source, halves(first, rows)[i]]
            copy = on_y(ref, ref, which, 2 + i, offset)
            copy.start()
            sends.append(copy)

    def tensor_end(everyone, which, first=0, rows=ROWS):
        for i, offset in ((0, 1), (1, 3)):
            ref = everyone.at[across, halves(first, rows)[i]]
            on_y(ref, ref, which, 2 + i, offset).wait_recv()

    def holder(source):
        return lax.rem(source, 2) == lax.div(z, 4)

    def piece(i):
        dest = 4 * lax.rem(t, 2) + i
        target = slab.at[lax.div(t, 2), z]
        source = up.at[:, pl.ds(i * 256, 256)]
        device = (place.d, xh * NZ + dest, t)
        return dest, source, remote(source, target, send_sem.at[0], a_rs.at[z], device)

    def spread_pieces():
        for i in range(4):
            dest, source, copy = piece(i)

            @pl.when(dest != z)
            def _(copy=copy):
                copy.start()

            @pl.when(dest == z)
            def _(source=source):
                slab[lax.div(t, 2), z] = source[...]

    def pieces_sent():
        for i in range(4):
            dest, _, copy = piece(i)

            @pl.when(dest != z)
            def _(copy=copy):
                copy.wait_send()

    def slab_half(source, i):
        return slab.at[lax.div(source, 2), pl.ds(4 * i, 4)]

    def share_start():
        @pl.when(holder(t))
        def _():
            for i in range(1, NZ):
                source = lax.rem(z + i, NZ)
                ref = slab.at[lax.div(t, 2), source]
                remote(ref, ref, send_sem.at[0], a_rs.at[source], place.zdev(1)).wait_recv()
            ref = slab.at[lax.div(t, 2)]
            on_y(ref, ref, 2, 0, 1).start()
            on_y(ref, ref, 2, 1, 3).start()

    def share_forward():
        @pl.when(holder(before))
        def _():
            for i, offset, source in ((0, 1, before), (1, 3, after)):
                ref = slab.at[lax.div(source, 2)]
                on_y(ref, ref, 2, i, offset).wait_recv()
                ref = slab_half(source, i)
                on_y(ref, ref, 2, 2 + i, offset).start()

    def share_end():
        @pl.when(holder(across))
        def _():
            for i, offset in ((0, 1), (1, 3)):
                ref = slab_half(across, i)
                on_y(ref, ref, 2, 2 + i, offset).wait_recv()

    def share_sent():
        @pl.when(holder(t))
        def _():
            ref = slab.at[lax.div(t, 2)]
            on_y(ref, ref, 2, 0, 1).wait_send()
            on_y(ref, ref, 2, 1, 3).wait_send()

        @pl.when(holder(before))
        def _():
            for i, offset, source in ((0, 1, before), (1, 3, after)):
                ref = slab_half(source, i)
                on_y(ref, ref, 2, 2 + i, offset).wait_send()

    stores = []

    def store(src, dst):
        copy = pltpu.make_async_copy(src, dst, store_sem.at[len(stores)])
        copy.start()
        stores.append(copy)

    def cross_start(term, sbuf, rbuf, which):
        value = term(across).astype(BF16)
        for i, offset in ((0, 1), (1, 3)):
            part = halves(0, ROWS)[i]
            sbuf[0, part] = value[i * half : (i + 1) * half]
            copy = on_y(sbuf.at[0, part], rbuf.at[0, part], which, 2 + i, offset)
            copy.start()
            sends.append(copy)

    def cross_forward(term, sbuf, rbuf, which):
        for i, offset, dest in ((0, 1, after), (1, 3, before)):
            value = term(dest)
            part = halves(0, ROWS)[i]
            ref = rbuf.at[0, part]
            on_y(ref, ref, which, 2 + i, offset).wait_recv()
            rest = slice((1 - i) * half, (2 - i) * half)
            sbuf[1 + i, part] = (value[i * half : (i + 1) * half] + ref[...]).astype(BF16)
            sbuf[1 + i, halves(0, ROWS)[1 - i]] = value[rest].astype(BF16)
            copy = on_y(sbuf.at[1 + i], rbuf.at[1 + i], which, i, offset)
            copy.start()
            sends.append(copy)

    def cross_end(own, rbuf, which, out):
        value = own[...]
        for i, offset in ((0, 1), (1, 3)):
            ref = rbuf.at[1 + i]
            on_y(ref, ref, which, i, offset).wait_recv()
            value = value + ref[...]
        out[...] = value.astype(BF16)

    load_tok.wait()
    tensor_start(tok, tok_all, 0)
    load_up.wait()
    spread_pieces()
    position = lax.broadcasted_iota(jnp.int32, (ROWS, HEAD_SIZE), 0) + place.s * ROWS
    angles = position.astype(F32) * freqs[...]
    cosine[...] = jnp.cos(angles)
    low = lax.broadcasted_iota(jnp.int32, (ROWS, HEAD_SIZE), 1) < HEAD_SIZE // 2
    sines = jnp.sin(angles)
    sine[...] = jnp.where(low, -sines, sines)
    groups = exponents.shape[1]
    group = lax.broadcasted_iota(jnp.int32, (ROWS, groups), 0) // SCALE_TOKENS
    group = group + place.s * (ROWS // SCALE_TOKENS)
    pick = lax.broadcasted_iota(jnp.int32, (ROWS, groups), 1) == group
    expo[...] = dot(pick.astype(F32).astype(BF16), exponents[...].astype(F32).astype(BF16), 1, 1)
    row = lax.broadcasted_iota(jnp.int32, (PAIR, HEAD_SIZE), 0)
    key_place[...] = jnp.where(row < ROWS, row, row + (NZ - 1) * ROWS)
    limit[...] = place.s * ROWS + lax.rem(
        lax.broadcasted_iota(jnp.int32, (1, QROWS), 1), jnp.int32(ROWS)
    )
    top[...] = jnp.full(top.shape, -jnp.inf, F32)
    total[...] = jnp.zeros(total.shape, F32)
    acc[...] = jnp.zeros(acc.shape, F32)
    dq[...] = jnp.zeros(dq.shape, F32)

    @pl.when(xh == 1)
    def _():
        dkv_other[...] = jnp.zeros(dkv_other.shape, BF16)

    def weight_rows(source):
        return pl.ds(pl.multiple_of(source * WIDTH, WIDTH), WIDTH)

    def project_kv(source):
        return dot(tok_all[source], wq[weight_rows(source), 512:768], 1, 0)

    def project_q(source):
        return dot(tok_all[source], wq[weight_rows(source), 0:512], 1, 0)

    def around(step):
        return lax.rem(z + step + NZ, NZ)

    def forward(zk):
        keys = kv[0, zk]
        values = kv[1, zk]
        for cut in range(0, QROWS, HEAD_SIZE):
            cut = slice(cut, cut + HEAD_SIZE)
            scores = dot(keys, q[cut], 1, 1)
            allowed = key_place[...] <= limit[:, cut] - zk * ROWS
            scores = jnp.where(allowed, scores, -jnp.inf)
            before = top[:, cut]
            now = jnp.maximum(before, jnp.max(scores, axis=0, keepdims=True))
            weights = jnp.exp2((scores - now) * SCALE2)
            alpha = jnp.exp2((before - now) * SCALE2)
            top[:, cut] = now
            total[:, cut] = total[:, cut] * alpha + jnp.sum(weights, axis=0, keepdims=True)
            acc[:, cut] = acc[:, cut] * alpha + dot(values, weights.astype(BF16), 0, 0)

    def merged_term(source):
        return dot(up_all[source], wo[:, weight_rows(source)], 1, 1)

    c, s = cosine[...], sine[...]

    def kv_part(column, i):
        def part(step, di, at):
            first = column * ROWS
            rows = pl.ds(pl.multiple_of(first, ROWS), ROWS)
            if step == 4:
                rows = pl.ds(pl.multiple_of(first + di * half, half), half)
            return kv.at[i, lax.rem(at + 2 * NZ, NZ), rows]

        return part

    own_rings = [gather_ring(place, kv_part(xh, i), i, send_sem, ag_rs, sends) for i in range(2)]
    other_rings = [
        gather_ring(place, kv_part(1 - xh, i), 2 + i, send_sem, ag_rs, sends, 2) for i in range(2)
    ]

    def step_kv(i):
        run(own_rings[i], 1)
        run(other_rings[i], 1)

    for load in loads:
        load.wait()
    projected = project_kv(t)
    tensor_forward(tok_all, 0)
    projected = projected + project_kv(before) + project_kv(after)
    tensor_end(tok_all, 0)
    tensor_start(up, up_all, 1)
    projected = projected + project_kv(across)
    rows = pl.ds(pl.multiple_of(xh * ROWS, ROWS), ROWS)
    kv[0, z, rows] = turn(projected[:, 0:128], c, s).astype(BF16)
    kv[1, z, rows] = projected[:, 128:256].astype(BF16)
    for i in range(2):
        own = kv.at[i, z, rows]
        run(own_rings[i], 1)
        for di, sign in ((0, 1), (1, -1)):
            copy = remote(
                own, own, send_sem.at[0], ag_rs.at[2 + i, di, 0], place.diagonal(sign)
            )
            copy.start()
            sends.append(copy)
        swap(own, own, (0, 14)[i])
    projected = project_q(t) + project_q(before) + project_q(after) + project_q(across)
    for h in range(QUERY_PER_KEY):
        q[pl.ds(h * ROWS, ROWS)] = turn(
            projected[:, h * HEAD_SIZE : (h + 1) * HEAD_SIZE], c, s
        ).astype(BF16)
    step_kv(0)
    step_kv(1)
    for i in range(2):
        other = kv_part(1 - xh, i)(1, 0, z)
        sem = (0, 14)[i]
        remote(other, other, send_sem.at[0], x_rs.at[sem], place.xdev()).wait_recv()
    x_tok = [swap(tok_all.at[2 * (1 - xh) + i], tok_other.at[i], 1 + i) for i in range(2)]
    forward(z)
    forward(around(1))
    step_kv(0)
    forward(around(-1))
    step_kv(1)
    forward(around(2))
    tensor_forward(up_all, 1)
    load_wo.wait()
    grad = merged_term(t) + merged_term(before)
    step_kv(0)
    forward(around(-2))
    step_kv(1)
    forward(around(3))
    grad = grad + merged_term(after)
    run(own_rings[0])
    run(other_rings[0])
    forward(around(-3))
    run(own_rings[1])
    run(other_rings[1])
    forward(around(4))

    out_t = (acc[...] / total[...]).astype(BF16)
    out = out_t.astype(F32).T.astype(BF16)
    for h in range(QUERY_PER_KEY):
        rows = out[h * ROWS : (h + 1) * ROWS]
        merged[:, h * HEAD_SIZE : (h + 1) * HEAD_SIZE] = rows
        merged_all[h // 2, z, :, (h % 2) * HEAD_SIZE : (h % 2 + 1) * HEAD_SIZE] = rows

    def merged_part(h):
        def part(step, di, at):
            ref = merged_all.at[h, lax.rem(at + 2 * NZ, NZ)]
            return ref.at[pl.ds(di * (ROWS // 2), ROWS // 2)] if step == 4 else ref

        return part

    merged_rings = [
        gather_ring(place, merged_part(h), h, send_sem, m_rs, sends) for h in range(2)
    ]

    def step_merged():
        for ring in merged_rings:
            run(ring, 1)

    step_merged()
    tensor_end(up_all, 1)
    grad = grad + merged_term(across)
    for h in range(QUERY_PER_KEY):
        do[pl.ds(h * ROWS, ROWS)] = grad[:, h * HEAD_SIZE : (h + 1) * HEAD_SIZE].astype(BF16)
    logsum[...] = top[...] * SCALE2 + jnp.log2(total[...])
    delta[...] = jnp.sum(do[...].astype(F32).T * out_t.astype(F32), axis=0, keepdims=True)

    def give_dkv(slot):
        return remote(
            dkv.at[slot, 0], dkv_other.at[slot], send_sem.at[0], x_rs.at[6 + slot], place.xdev()
        )

    def cross_dkv(slots):
        @pl.when(xh == 1)
        def _():
            for slot in slots:
                give_dkv(slot).start()

    def backward(slot, zk):
        keys = kv[0, zk]
        values = kv[1, zk]
        scores = dot(keys, q[...], 1, 1)
        allowed = key_place[:, 0:1] <= limit[...] - zk * ROWS
        probs = jnp.exp2(jnp.where(allowed, scores * SCALE2 - logsum[...], -jnp.inf))
        grad_probs = dot(values, do[...], 1, 1)
        grad_scores = (probs * (grad_probs - delta[...])).astype(BF16)
        dv = dot(probs.astype(BF16), do[...], 1, 0).astype(BF16)
        dk = (dot(grad_scores, q[...], 1, 0) * SCALE).astype(BF16)
        dq[...] += dot(keys, grad_scores, 0, 0)
        for column in range(2):
            rows = slice(column * ROWS, (column + 1) * ROWS)
            dkv[slot, column, 0:ROWS] = dk[rows]
            dkv[slot, column, ROWS:PAIR] = dv[rows]

    kv_here = set()

    def kv_term(step, di):
        slot = {4: 0, 3: 1, 2: 3, 1: 5, 0: 7}[step] + (di if step in (1, 2, 3) else 0)
        if slot not in kv_here:
            kv_here.add(slot)

            @pl.when(xh == 0)
            def _():
                give_dkv(slot).wait_recv()

        return dkv[slot, xh].astype(F32) + dkv_other[slot].astype(F32)

    ring_kv = TwoStages(place, PAIR, kv_term, kv_sb, kv_rb, send_sem, kv_rs, sends)

    def attended_term(dest):
        return dot(merged[...], wo[:, pl.ds(pl.multiple_of(dest * WIDTH, WIDTH), WIDTH)], 1, 0)

    def columns(dest):
        return pl.ds(pl.multiple_of(lax.rem(dest, 4) * 256, 256), 256)

    def load_q(dest, sub, part, step, di, width=256, first=0):
        shard = lax.div(dest, 4)
        left = tok_all[2 * xh + shard, :, columns(dest)]
        left_other = tok_other[shard, :, columns(dest)]
        if part is not None:
            left = left[:, part * 128 : (part + 1) * 128]
            left_other = left_other[:, part * 128 : (part + 1) * 128]
        cut = slice(first + sub * width, first + (sub + 1) * width)
        return dot(left, gqkv[0, :, cut], 0, 0) + dot(left_other, gqkv[1, :, cut], 0, 0)

    def done_q(sub, value):
        cut = pl.ds(sub * 256, 256)
        gwq[sub] = value.astype(BF16)
        store(gwq.at[sub], gwq_hbm.at[:, cut])

    ring_q = scatter_ring(place, (0, 1), 256, load_q, q_sb, q_rb, send_sem, q_rs, sends, done_q)

    def load_k(dest, sub, part, step, di):
        return load_q(dest, sub, part, step, di, 128, 512)

    def done_k(sub, value):
        cut = pl.ds(sub * 128, 128)
        gwq[2, :, cut] = value.astype(BF16)
        store(gwq.at[2, :, cut], gwq_hbm.at[:, pl.ds(512 + sub * 128, 128)])

    ring_k = scatter_ring(place, (0, 1), 256, load_k, k_sb, k_rb, send_sem, k_rs, sends, done_k)

    def squeeze(value, column):
        e = expo[:, column : column + 1]
        sent = jnp.clip(value * jnp.exp2(-e), -127.0, 127.0).astype(BF16)
        return sent.astype(F32) * jnp.exp2(e)

    share_start()
    backward(0, around(4))
    backward(1, around(3))
    backward(2, around(-3))
    cross_dkv((0, 1, 2))
    backward(3, around(2))
    backward(4, around(-2))
    step_merged()
    backward(5, around(1))
    backward(6, around(-1))
    backward(7, z)
    grad = dq[...].T * SCALE
    x_gq = []
    for h in range(QUERY_PER_KEY):
        gqkv[0, :, h * HEAD_SIZE : (h + 1) * HEAD_SIZE] = turn(
            squeeze(grad[h * ROWS : (h + 1) * ROWS], h), c, -s
        ).astype(BF16)
        if h % 2:
            cut = pl.ds((h - 1) * HEAD_SIZE, 2 * HEAD_SIZE)
            sem = (4, 15)[h // 2]
            x_gq.append(swap(gqkv.at[0, :, cut], gqkv.at[1, :, cut], sem))
    cross_dkv((3, 4, 5, 6, 7))
    step_merged()
    ring_kv.far()
    cross_start(attended_term, att_s, att_r, 3)
    for copy in x_tok:
        copy.wait_recv()
    x_gq[0].wait_recv()
    run(ring_q, 1)
    x_gq[1].wait_recv()
    run(ring_q, 1)
    step_merged()
    ring_kv.middle()
    ring_kv.near()
    share_forward()
    run(ring_q, 2)
    kv_sum = ring_kv.end()
    gqkv[0, :, 512:640] = turn(squeeze(kv_sum[:ROWS], 4), c, -s).astype(BF16)
    gqkv[0, :, 640:768] = squeeze(kv_sum[ROWS:], 5).astype(BF16)
    x_gkv = swap(gqkv.at[0, :, pl.ds(512, 256)], gqkv.at[1, :, pl.ds(512, 256)], 5)

    def tokens_term(dest):
        return dot(gqkv[0], wq[pl.ds(pl.multiple_of(dest * WIDTH, WIDTH), WIDTH)], 1, 1)

    cross_forward(attended_term, att_s, att_r, 3)
    cross_start(tokens_term, tok_s, tok_r, 4)
    run(ring_q, 2)
    x_gkv.wait_recv()
    run(ring_k, 2)
    for ring in merged_rings:
        run(ring)
    share_end()

    def out_term(h, column):
        tokens = NZ * ROWS
        return dot(
            merged_all[h].reshape(tokens, 256), slab[column].reshape(tokens, 256), 0, 0
        )

    for h in range(2):
        o_sb[pl.ds(h * 256, 256)] = out_term(h, 1 - xh).astype(BF16)
    x_o = swap(o_sb, o_rb, 3)
    att_own[...] = attended_term(t)
    tok_own[...] = tokens_term(t)
    run(ring_k, 2)
    run(ring_q, 2)
    run(ring_k, 2)
    cross_forward(tokens_term, tok_s, tok_r, 4)
    cross_end(att_own, att_r, 3, attended)
    store(attended, attended_hbm)
    run(ring_q)
    run(ring_k, 2)
    x_o.wait_recv()
    for h in range(2):
        rows = pl.ds(h * 256, 256)
        gwo[rows] = (out_term(h, xh) + o_rb[rows]).astype(BF16)
    store(gwo, gwo_hbm)
    cross_end(tok_own, tok_r, 4, grad_tokens)
    store(grad_tokens, grad_tokens_hbm)
    run(ring_k)
    pieces_sent()

    @pl.when(xh == 1)
    def _():
        for slot in range(NZ):
            give_dkv(slot).wait_send()

    share_sent()
    for copy in sends:
        copy.wait_send()
    for copy in stores:
        copy.wait()


def layer(tok, up, wq, wo, freqs, exponents):
    vmem = pl.BlockSpec(memory_space=pltpu.VMEM)
    hbm = pl.BlockSpec(memory_space=pl.ANY)
    shape = jax.ShapeDtypeStruct
    dma = pltpu.SemaphoreType.DMA
    buf = pltpu.VMEM
    heads = QUERY_PER_KEY * HEAD_SIZE
    return pl.pallas_call(
        layer_kernel,
        name="layer",
        out_shape=[
            shape((ROWS, WIDTH), BF16),
            shape((ROWS, WIDTH), BF16),
            shape((256, 768), BF16),
            shape((512, 256), BF16),
        ],
        in_specs=[hbm, hbm, hbm, hbm, vmem, vmem],
        out_specs=[hbm] * 4,
        scratch_shapes=[
            buf(wq.shape, BF16),
            buf(wo.shape, BF16),
            buf((NT, ROWS, WIDTH), BF16),
            buf((NT, ROWS, WIDTH), BF16),
            buf((2, ROWS, WIDTH), BF16),
            buf((2, NZ, ROWS, 256), BF16),
            buf((ROWS, HEAD_SIZE), F32),
            buf((ROWS, HEAD_SIZE), F32),
            buf((ROWS, 6), F32),
            buf((QROWS, HEAD_SIZE), BF16),
            buf((2, NZ, PAIR, HEAD_SIZE), BF16),
            buf((QROWS, HEAD_SIZE), BF16),
            buf((ROWS, heads), BF16),
            buf((2, NZ, ROWS, 256), BF16),
            buf((2, ROWS, 768), BF16),
            buf((PAIR, HEAD_SIZE), jnp.int32),
            buf((1, QROWS), jnp.int32),
            buf((1, QROWS), F32),
            buf((1, QROWS), F32),
            buf((HEAD_SIZE, QROWS), F32),
            buf((1, QROWS), F32),
            buf((1, QROWS), F32),
            buf((HEAD_SIZE, QROWS), F32),
            buf((NZ, 2, PAIR, HEAD_SIZE), BF16),
            buf((NZ, PAIR, HEAD_SIZE), BF16),
            buf((ROWS, WIDTH), F32),
            buf((3, ROWS, WIDTH), BF16),
            buf((3, ROWS, WIDTH), BF16),
            buf((ROWS, WIDTH), F32),
            buf((3, ROWS, WIDTH), BF16),
            buf((3, ROWS, WIDTH), BF16),
            buf((2, 4, PAIR, HEAD_SIZE), BF16),
            buf((2, 4, PAIR, HEAD_SIZE), BF16),
            buf((512, 256), BF16),
            buf((512, 256), BF16),
            buf((2, 4, 2, 256, 256), BF16),
            buf((2, 4, 2, 256, 256), BF16),
            buf((2, 4, 2, 256, 128), BF16),
            buf((2, 4, 2, 256, 128), BF16),
            buf((ROWS, WIDTH), BF16),
            buf((ROWS, WIDTH), BF16),
            buf((3, 256, 256), BF16),
            buf((512, 256), BF16),
            dma((7,)),
            dma((7,)),
            dma((1,)),
            dma((5, 4)),
            dma((16,)),
            dma((4, 2, 4)),
            dma((2, 4)),
            dma((2, 2, 4)),
            dma((NZ,)),
            dma((2, 4, 2)),
            dma((2, 4, 2)),
        ],
        compiler_params=pltpu.CompilerParams(
            collective_id=0, has_side_effects=True, vmem_limit_bytes=VMEM_LIMIT
        ),
    )(tok, up, wq, wo, freqs, exponents)


def settle_kernel(*refs):
    number = (len(refs) - 1) // 3
    sources, targets, held, sems = (
        refs[:number],
        refs[number : 2 * number],
        refs[2 * number : 3 * number],
        refs[-1],
    )
    for i in range(number):
        pltpu.make_async_copy(sources[i], held[i], sems.at[0, i]).start()
    for i in range(number):
        pltpu.make_async_copy(sources[i], held[i], sems.at[0, i]).wait()
        pltpu.make_async_copy(held[i], targets[i], sems.at[1, i]).start()
    for i in range(number):
        pltpu.make_async_copy(held[i], targets[i], sems.at[1, i]).wait()


def settle(*arrays):
    hbm = pl.BlockSpec(memory_space=pl.ANY)
    return pl.pallas_call(
        settle_kernel,
        name="settle",
        out_shape=[jax.ShapeDtypeStruct(a.shape, a.dtype) for a in arrays],
        in_specs=[hbm] * len(arrays),
        out_specs=[hbm] * len(arrays),
        scratch_shapes=[pltpu.VMEM(a.shape, a.dtype) for a in arrays]
        + [pltpu.SemaphoreType.DMA((2, len(arrays)))],
        compiler_params=pltpu.CompilerParams(vmem_limit_bytes=VMEM_LIMIT),
    )(*arrays)


def local(tokens, input_projection_weight, w_out, upstream, exponents):
    half = HEAD_SIZE // 2
    freqs = np.power(np.float32(THETA), -np.arange(half, dtype=np.float32) * 2.0 / HEAD_SIZE)
    freqs = jnp.asarray(np.tile(freqs, 2).reshape(1, HEAD_SIZE), F32)
    return settle(
        *layer(tokens, upstream, input_projection_weight, w_out, freqs, exponents.T)
    )


def solution(mesh):
    in_specs = (
        P(("dp", "seq"), "tensor"),
        P(None, "tensor"),
        P("tensor", None),
        P(("dp", "seq"), "tensor"),
        P("dp", "tensor"),
    )
    out_specs = (
        P(("dp", "seq"), "tensor"),
        P(("dp", "seq"), "tensor"),
        P(("dp", "seq"), "tensor"),
        P(("dp", "tensor"), "seq"),
    )
    return jax.shard_map(local, mesh=mesh, in_specs=in_specs, out_specs=out_specs, check_vma=False)
```

```python
import functools
import math

import jax
import jax.numpy as jnp
import numpy as np
from jax import lax
from jax.experimental import pallas as pl
from jax.experimental.pallas import tpu as pltpu
from jax.sharding import PartitionSpec as P

HEAD_SIZE = 128
QUERY_PER_KEY = 4
SCALE_TOKENS = 16
THETA = 500000.0

NZ = 8
NT = 4
ROWS = 192
QROWS = QUERY_PER_KEY * ROWS
PAIR = 2 * ROWS
WIDTH = 1024
MESH = pl.DeviceIdType.MESH
BF16 = jnp.bfloat16
F32 = jnp.float32
SCALE = 1.0 / math.sqrt(HEAD_SIZE)
SCALE2 = SCALE * math.log2(math.e)
VMEM_LIMIT = 60 * 2**20


def dot(left, right, left_dim, right_dim):
    return lax.dot_general(
        left, right, (((left_dim,), (right_dim,)), ((), ())), preferred_element_type=F32
    )


class Place:
    def __init__(self):
        self.d = lax.axis_index("dp")
        self.s = lax.axis_index("seq")
        self.t = lax.axis_index("tensor")
        self.xh = lax.div(self.s, NZ)
        self.z = lax.rem(self.s, NZ)

    def tensor(self, offset):
        return (self.d, self.s, lax.rem(self.t + offset, NT))

    def zdev(self, sign):
        return (self.d, self.xh * NZ + lax.rem(self.z + sign + NZ, NZ), self.t)

    def xdev(self):
        return (self.d, (1 - self.xh) * NZ + self.z, self.t)

    def diagonal(self, sign):
        return (self.d, (1 - self.xh) * NZ + lax.rem(self.z + sign + NZ, NZ), self.t)

    def enter(self):
        barrier = pltpu.get_barrier_semaphore()
        partners = [self.tensor(1), self.tensor(3)]
        partners += [self.zdev(i) for i in range(1, NZ)] + [self.xdev()]
        partners += [self.diagonal(1), self.diagonal(-1)]
        for partner in partners:
            pl.semaphore_signal(barrier, inc=1, device_id=partner, device_id_type=MESH)
        pl.semaphore_wait(barrier, len(partners))


def remote(src, dst, send_sem, recv_sem, device):
    return pltpu.make_async_remote_copy(
        src_ref=src,
        dst_ref=dst,
        send_sem=send_sem,
        recv_sem=recv_sem,
        device_id=device,
        device_id_type=MESH,
    )


def turn(vectors, cosine, sine):
    return vectors * cosine + pltpu.roll(vectors, HEAD_SIZE // 2, 1) * sine


def gather_ring(place, part, which, ss, rs, sends, first=1):
    def arrived(step, di, sign):
        ref = part(step, di, place.z - sign * step)
        sem = rs.at[which, di, step - 1]
        remote(ref, ref, ss.at[0], sem, place.zdev(sign)).wait_recv()

    for step in range(first, 5):
        for di, sign in ((0, 1), (1, -1)):
            if step > 1:
                arrived(step - 1, di, sign)
            ref = part(step, di, place.z - sign * (step - 1))
            copy = remote(
                ref,
                ref,
                ss.at[0],
                rs.at[which, di, step - 1],
                place.zdev(sign),
            )
            copy.start()
            sends.append(copy)
        yield
    for di, sign in ((0, 1), (1, -1)):
        arrived(4, di, sign)


def scatter_ring(place, subs, rows, load, sbuf, rbuf, ss, rs, sends, done):
    half = rows // 2
    for step in (4, 3, 2, 1):
        for sub in subs:
            for di, sign in ((0, 1), (1, -1)):
                dest = lax.rem(place.z + sign * step + NZ, NZ)
                cut = pl.ds(di * half, half)
                here = sbuf.at[di, step - 1, sub]
                there = rbuf.at[di, step - 1, sub]
                if step == 4:
                    here, there = here.at[cut], there.at[cut]
                    here[...] = load(dest, sub, di, step, di).astype(BF16)
                else:
                    value = load(dest, sub, None, step, di)
                    before = rbuf.at[di, step, sub]
                    if step == 3:
                        before = before.at[cut]
                    remote(
                        before, before, ss.at[0], rs.at[di, step, sub], place.zdev(sign)
                    ).wait_recv()
                    if step == 3:
                        here[cut] = (value[di * half : (di + 1) * half] + before[...]).astype(BF16)
                        rest = 1 - di
                        here[pl.ds(rest * half, half)] = value[
                            rest * half : (rest + 1) * half
                        ].astype(BF16)
                    else:
                        here[...] = (value + before[...]).astype(BF16)
                copy = remote(
                    here, there, ss.at[0], rs.at[di, step - 1, sub], place.zdev(sign)
                )
                copy.start()
                sends.append(copy)
            yield
    for sub in subs:
        total = load(place.z, sub, None, 0, 0)
        for di, sign in ((0, 1), (1, -1)):
            ref = rbuf.at[di, 0, sub]
            remote(ref, ref, ss.at[0], rs.at[di, 0, sub], place.zdev(sign)).wait_recv()
            total = total + ref[...]
        done(sub, total)


def run(steps, count=None):
    if count is None:
        for _ in steps:
            pass
    else:
        for _ in range(count):
            next(steps)


class TwoStages:
    def __init__(self, place, rows, term, sbuf, rbuf, ss, rs, sends):
        self.place, self.half, self.term, self.sends = place, rows // 2, term, sends
        self.refs = sbuf, rbuf, ss, rs

    def copy(self, di, step, hops):
        sbuf, rbuf, ss, rs = self.refs
        at = (di, step - 1)
        here, there = sbuf.at[at], rbuf.at[at]
        if step == 4:
            cut = pl.ds(di * self.half, self.half)
            here, there = here.at[cut], there.at[cut]
        return remote(here, there, ss.at[0], rs.at[at], self.place.zdev(hops))

    def send(self, di, step, hops, value):
        sbuf = self.refs[0]
        if step == 4:
            cut = slice(di * self.half, (di + 1) * self.half)
            sbuf[di, step - 1, cut] = value[cut].astype(BF16)
        else:
            sbuf[di, step - 1] = value.astype(BF16)
        copy = self.copy(di, step, hops)
        copy.start()
        self.sends.append(copy)

    def far(self):
        value = self.term(4, 0)
        for di, sign in ((0, 1), (1, -1)):
            self.send(di, 3, sign, self.term(3, di))
            self.send(di, 4, 2 * sign, value)

    def near(self):
        for di, sign in ((0, 1), (1, -1)):
            self.send(di, 1, sign, self.term(1, di))

    def middle(self):
        half, (_, rbuf, _, _) = self.half, self.refs
        for di, sign in ((0, 1), (1, -1)):
            value = self.term(2, di)
            self.copy(di, 3, sign).wait_recv()
            self.copy(di, 4, 2 * sign).wait_recv()
            value = value + rbuf[di, 2]
            parts = [value[:half], value[half:]]
            parts[di] = parts[di] + rbuf[di, 3, di * half : (di + 1) * half]
            self.send(di, 2, 2 * sign, jnp.concatenate(parts, axis=0))

    def end(self):
        value = self.term(0, 0)
        for di, sign in ((0, 1), (1, -1)):
            for step in (1, 2):
                self.copy(di, step, step * sign).wait_recv()
                value = value + self.refs[1][di, step - 1]
        return value


def layer_kernel(
    tok_hbm, up_hbm, wq_hbm, wo_hbm, freqs, exponents,
    attended_hbm, grad_tokens_hbm, gwq_hbm, gwo_hbm,
    wq, wo, tok_all, up_all, tok_other, slab, cosine, sine, expo,
    q, kv, do, merged, merged_all, gqkv,
    key_place, limit, top, total, acc, logsum, delta, dq,
    dkv, dkv_other,
    att_own, att_s, att_r, tok_own, tok_s, tok_r,
    kv_sb, kv_rb, o_sb, o_rb, q_sb, q_rb, k_sb, k_rb,
    attended, grad_tokens, gwq, gwo,
    load_sem, store_sem, send_sem, y_rs, x_rs, ag_rs,
    kv_rs, m_rs, a_rs, q_rs, k_rs,
):
    place = Place()
    t, xh, z = place.t, place.xh, place.z
    tok, up = tok_all.at[t], up_all.at[t]
    load_tok = pltpu.make_async_copy(tok_hbm, tok, load_sem.at[5])
    load_tok.start()
    load_up = pltpu.make_async_copy(up_hbm, up, load_sem.at[6])
    load_up.start()
    loads = []
    for i in range(NT):
        rows = pl.ds(pl.multiple_of(lax.rem(t + (0, 1, 3, 2)[i], NT) * WIDTH, WIDTH), WIDTH)
        loads.append(pltpu.make_async_copy(wq_hbm.at[rows], wq.at[rows], load_sem.at[i]))
        loads[-1].start()
    load_wo = pltpu.make_async_copy(wo_hbm, wo, load_sem.at[4])
    load_wo.start()
    place.enter()
    sends = []
    half = ROWS // 2

    def swap(src, dst, i):
        copy = remote(src, dst, send_sem.at[0], x_rs.at[i], place.xdev())
        copy.start()
        sends.append(copy)
        return copy

    def on_y(src, dst, which, i, offset):
        return remote(src, dst, send_sem.at[0], y_rs.at[which, i], place.tensor(offset))

    before, after, across = (lax.rem(t + i, NT) for i in (3, 1, 2))

    def halves(first, rows):
        return pl.ds(first, rows // 2), pl.ds(first + rows // 2, rows // 2)

    def tensor_start(everyone, which):
        for rest in range(2):
            for i, offset in ((0, 1), (1, 3)):
                ref = everyone.at[t, halves(0, ROWS)[(i + rest) % 2]]
                copy = on_y(ref, ref, which, i + 4 * rest, offset)
                copy.start()
                sends.append(copy)

    def tensor_forward(everyone, which):
        for i, offset, source in ((0, 1, before), (1, 3, after)):
            ref = everyone.at[source, halves(0, ROWS)[i]]
            on_y(ref, ref, which, i, offset).wait_recv()
            copy = on_y(ref, ref, which, 2 + i, offset)
            copy.start()
            sends.append(copy)

    def tensor_rest(everyone, which):
        for i, offset, source in ((0, 1, before), (1, 3, after)):
            ref = everyone.at[source, halves(0, ROWS)[1 - i]]
            on_y(ref, ref, which, 4 + i, offset).wait_recv()

    def tensor_end(everyone, which):
        for i, offset in ((0, 1), (1, 3)):
            ref = everyone.at[across, halves(0, ROWS)[i]]
            on_y(ref, ref, which, 2 + i, offset).wait_recv()

    def holder(source):
        return lax.rem(source, 2) == lax.div(z, 4)

    def piece(i):
        dest = 4 * lax.rem(t, 2) + i
        target = slab.at[lax.div(t, 2), z]
        source = up.at[:, pl.ds(i * 256, 256)]
        device = (place.d, xh * NZ + dest, t)
        return dest, source, remote(source, target, send_sem.at[0], a_rs.at[z], device)

    def spread_pieces():
        for i in range(4):
            dest, source, copy = piece(i)

            @pl.when(dest != z)
            def _(copy=copy):
                copy.start()

            @pl.when(dest == z)
            def _(source=source):
                slab[lax.div(t, 2), z] = source[...]

    def pieces_sent():
        for i in range(4):
            dest, _, copy = piece(i)

            @pl.when(dest != z)
            def _(copy=copy):
                copy.wait_send()

    def slab_half(source, i):
        return slab.at[lax.div(source, 2), pl.ds(4 * i, 4)]

    def share_start():
        @pl.when(holder(t))
        def _():
            for i in range(1, NZ):
                source = lax.rem(z + i, NZ)
                ref = slab.at[lax.div(t, 2), source]
                remote(ref, ref, send_sem.at[0], a_rs.at[source], place.zdev(1)).wait_recv()
            ref = slab.at[lax.div(t, 2)]
            on_y(ref, ref, 2, 0, 1).start()
            on_y(ref, ref, 2, 1, 3).start()

    def share_forward():
        @pl.when(holder(before))
        def _():
            for i, offset, source in ((0, 1, before), (1, 3, after)):
                ref = slab.at[lax.div(source, 2)]
                on_y(ref, ref, 2, i, offset).wait_recv()
                ref = slab_half(source, i)
                on_y(ref, ref, 2, 2 + i, offset).start()

    def share_end():
        @pl.when(holder(across))
        def _():
            for i, offset in ((0, 1), (1, 3)):
                ref = slab_half(across, i)
                on_y(ref, ref, 2, 2 + i, offset).wait_recv()

    def share_sent():
        @pl.when(holder(t))
        def _():
            ref = slab.at[lax.div(t, 2)]
            on_y(ref, ref, 2, 0, 1).wait_send()
            on_y(ref, ref, 2, 1, 3).wait_send()

        @pl.when(holder(before))
        def _():
            for i, offset, source in ((0, 1, before), (1, 3, after)):
                ref = slab_half(source, i)
                on_y(ref, ref, 2, 2 + i, offset).wait_send()

    stores = []

    def store(src, dst):
        copy = pltpu.make_async_copy(src, dst, store_sem.at[len(stores)])
        copy.start()
        stores.append(copy)

    def cross_start(term, sbuf, rbuf, which):
        value = term(across).astype(BF16)
        for i, offset in ((0, 1), (1, 3)):
            part = halves(0, ROWS)[i]
            sbuf[0, part] = value[i * half : (i + 1) * half]
            copy = on_y(sbuf.at[0, part], rbuf.at[0, part], which, 2 + i, offset)
            copy.start()
            sends.append(copy)

    def cross_forward(term, sbuf, rbuf, which):
        for i, offset, dest in ((0, 1, after), (1, 3, before)):
            value = term(dest)
            part = halves(0, ROWS)[i]
            ref = rbuf.at[0, part]
            on_y(ref, ref, which, 2 + i, offset).wait_recv()
            rest = slice((1 - i) * half, (2 - i) * half)
            sbuf[1 + i, part] = (value[i * half : (i + 1) * half] + ref[...]).astype(BF16)
            sbuf[1 + i, halves(0, ROWS)[1 - i]] = value[rest].astype(BF16)
            copy = on_y(sbuf.at[1 + i], rbuf.at[1 + i], which, i, offset)
            copy.start()
            sends.append(copy)

    def cross_end(own, rbuf, which, out):
        value = own[...]
        for i, offset in ((0, 1), (1, 3)):
            ref = rbuf.at[1 + i]
            on_y(ref, ref, which, i, offset).wait_recv()
            value = value + ref[...]
        out[...] = value.astype(BF16)

    load_tok.wait()
    tensor_start(tok_all, 0)
    load_up.wait()
    spread_pieces()
    position = lax.broadcasted_iota(jnp.int32, (ROWS, HEAD_SIZE), 0) + place.s * ROWS
    angles = position.astype(F32) * freqs[...]
    cosine[...] = jnp.cos(angles)
    low = lax.broadcasted_iota(jnp.int32, (ROWS, HEAD_SIZE), 1) < HEAD_SIZE // 2
    sines = jnp.sin(angles)
    sine[...] = jnp.where(low, -sines, sines)
    groups = exponents.shape[1]
    group = lax.broadcasted_iota(jnp.int32, (ROWS, groups), 0) // SCALE_TOKENS
    group = group + place.s * (ROWS // SCALE_TOKENS)
    pick = lax.broadcasted_iota(jnp.int32, (ROWS, groups), 1) == group
    expo[...] = dot(pick.astype(F32).astype(BF16), exponents[...].astype(F32).astype(BF16), 1, 1)
    row = lax.broadcasted_iota(jnp.int32, (PAIR, HEAD_SIZE), 0)
    key_place[...] = jnp.where(row < ROWS, row, row + (NZ - 1) * ROWS)
    limit[...] = place.s * ROWS + lax.rem(
        lax.broadcasted_iota(jnp.int32, (1, QROWS), 1), jnp.int32(ROWS)
    )
    top[...] = jnp.full(top.shape, -jnp.inf, F32)
    total[...] = jnp.zeros(total.shape, F32)
    acc[...] = jnp.zeros(acc.shape, F32)
    dq[...] = jnp.zeros(dq.shape, F32)

    @pl.when(xh == 1)
    def _():
        dkv_other[...] = jnp.zeros(dkv_other.shape, BF16)

    def weight_rows(source):
        return pl.ds(pl.multiple_of(source * WIDTH, WIDTH), WIDTH)

    def project_kv(source):
        return dot(tok_all[source], wq[weight_rows(source), 512:768], 1, 0)

    def project_q(source):
        return dot(tok_all[source], wq[weight_rows(source), 0:512], 1, 0)

    def around(step):
        return lax.rem(z + step + NZ, NZ)

    def forward(zk):
        keys = kv[0, zk]
        values = kv[1, zk]
        for cut in range(0, QROWS, HEAD_SIZE):
            cut = slice(cut, cut + HEAD_SIZE)
            scores = dot(keys, q[cut], 1, 1)
            allowed = key_place[...] <= limit[:, cut] - zk * ROWS
            scores = jnp.where(allowed, scores, -jnp.inf)
            before = top[:, cut]
            now = jnp.maximum(before, jnp.max(scores, axis=0, keepdims=True))
            weights = jnp.exp2((scores - now) * SCALE2)
            alpha = jnp.exp2((before - now) * SCALE2)
            top[:, cut] = now
            total[:, cut] = total[:, cut] * alpha + jnp.sum(weights, axis=0, keepdims=True)
            acc[:, cut] = acc[:, cut] * alpha + dot(values, weights.astype(BF16), 0, 0)

    def merged_term(source):
        return dot(up_all[source], wo[:, weight_rows(source)], 1, 1)

    c, s = cosine[...], sine[...]

    def kv_part(column, i):
        def part(step, di, at):
            first = column * ROWS
            rows = pl.ds(pl.multiple_of(first, ROWS), ROWS)
            if step == 4:
                rows = pl.ds(pl.multiple_of(first + di * half, half), half)
            return kv.at[i, lax.rem(at + 2 * NZ, NZ), rows]

        return part

    own_rings = [gather_ring(place, kv_part(xh, i), i, send_sem, ag_rs, sends) for i in range(2)]
    other_rings = [
        gather_ring(place, kv_part(1 - xh, i), 2 + i, send_sem, ag_rs, sends, 2) for i in range(2)
    ]

    def step_kv(i):
        run(own_rings[i], 1)
        run(other_rings[i], 1)

    for load in loads:
        load.wait()
    projected = project_kv(t)
    tensor_forward(tok_all, 0)
    tensor_rest(tok_all, 0)
    projected = projected + project_kv(before) + project_kv(after)
    tensor_end(tok_all, 0)
    tensor_start(up_all, 1)
    projected = projected + project_kv(across)
    rows = pl.ds(pl.multiple_of(xh * ROWS, ROWS), ROWS)
    kv[0, z, rows] = turn(projected[:, 0:128], c, s).astype(BF16)
    kv[1, z, rows] = projected[:, 128:256].astype(BF16)
    for i in range(2):
        own = kv.at[i, z, rows]
        run(own_rings[i], 1)
        for di, sign in ((0, 1), (1, -1)):
            copy = remote(
                own, own, send_sem.at[0], ag_rs.at[2 + i, di, 0], place.diagonal(sign)
            )
            copy.start()
            sends.append(copy)
        swap(own, own, (0, 14)[i])
    projected = project_q(t) + project_q(before) + project_q(after) + project_q(across)
    for h in range(QUERY_PER_KEY):
        q[pl.ds(h * ROWS, ROWS)] = turn(
            projected[:, h * HEAD_SIZE : (h + 1) * HEAD_SIZE], c, s
        ).astype(BF16)
    step_kv(0)
    step_kv(1)
    for i in range(2):
        other = kv_part(1 - xh, i)(1, 0, z)
        sem = (0, 14)[i]
        remote(other, other, send_sem.at[0], x_rs.at[sem], place.xdev()).wait_recv()
    x_tok = [swap(tok_all.at[2 * (1 - xh) + i], tok_other.at[i], 1 + i) for i in range(2)]
    forward(z)
    forward(around(1))
    step_kv(0)
    forward(around(-1))
    step_kv(1)
    forward(around(2))
    tensor_forward(up_all, 1)
    tensor_rest(up_all, 1)
    load_wo.wait()
    grad = merged_term(t) + merged_term(before)
    step_kv(0)
    forward(around(-2))
    step_kv(1)
    forward(around(3))
    grad = grad + merged_term(after)
    run(own_rings[0])
    run(other_rings[0])
    forward(around(-3))
    run(own_rings[1])
    run(other_rings[1])
    forward(around(4))

    out_t = (acc[...] / total[...]).astype(BF16)
    out = out_t.astype(F32).T.astype(BF16)
    for h in range(QUERY_PER_KEY):
        rows = out[h * ROWS : (h + 1) * ROWS]
        merged[:, h * HEAD_SIZE : (h + 1) * HEAD_SIZE] = rows
        merged_all[h // 2, z, :, (h % 2) * HEAD_SIZE : (h % 2 + 1) * HEAD_SIZE] = rows

    def merged_part(h):
        def part(step, di, at):
            ref = merged_all.at[h, lax.rem(at + 2 * NZ, NZ)]
            return ref.at[pl.ds(di * (ROWS // 2), ROWS // 2)] if step == 4 else ref

        return part

    merged_rings = [
        gather_ring(place, merged_part(h), h, send_sem, m_rs, sends) for h in range(2)
    ]

    def step_merged(h):
        run(merged_rings[h], 1)

    step_merged(0)
    step_merged(1)
    tensor_end(up_all, 1)
    grad = grad + merged_term(across)
    for h in range(QUERY_PER_KEY):
        do[pl.ds(h * ROWS, ROWS)] = grad[:, h * HEAD_SIZE : (h + 1) * HEAD_SIZE].astype(BF16)
    logsum[...] = top[...] * SCALE2 + jnp.log2(total[...])
    delta[...] = jnp.sum(do[...].astype(F32).T * out_t.astype(F32), axis=0, keepdims=True)

    def give_dkv(slot):
        return remote(
            dkv.at[slot, 0], dkv_other.at[slot], send_sem.at[0], x_rs.at[6 + slot], place.xdev()
        )

    def cross_dkv(slot):
        @pl.when(xh == 1)
        def _():
            give_dkv(slot).start()

    def backward(slot, zk):
        keys = kv[0, zk]
        values = kv[1, zk]
        scores = dot(keys, q[...], 1, 1)
        allowed = key_place[:, 0:1] <= limit[...] - zk * ROWS
        probs = jnp.exp2(jnp.where(allowed, scores * SCALE2 - logsum[...], -jnp.inf))
        grad_probs = dot(values, do[...], 1, 1)
        grad_scores = (probs * (grad_probs - delta[...])).astype(BF16)
        dv = dot(probs.astype(BF16), do[...], 1, 0).astype(BF16)
        dk = (dot(grad_scores, q[...], 1, 0) * SCALE).astype(BF16)
        dq[...] += dot(keys, grad_scores, 0, 0)
        for column in range(2):
            rows = slice(column * ROWS, (column + 1) * ROWS)
            dkv[slot, column, 0:ROWS] = dk[rows]
            dkv[slot, column, ROWS:PAIR] = dv[rows]
        cross_dkv(slot)

    kv_here = set()

    def kv_term(step, di):
        slot = {4: 0, 3: 1, 2: 3, 1: 5, 0: 7}[step] + (di if step in (1, 2, 3) else 0)
        if slot not in kv_here:
            kv_here.add(slot)

            @pl.when(xh == 0)
            def _():
                give_dkv(slot).wait_recv()

        return dkv[slot, xh].astype(F32) + dkv_other[slot].astype(F32)

    ring_kv = TwoStages(place, PAIR, kv_term, kv_sb, kv_rb, send_sem, kv_rs, sends)

    def attended_term(dest):
        return dot(merged[...], wo[:, pl.ds(pl.multiple_of(dest * WIDTH, WIDTH), WIDTH)], 1, 0)

    def columns(dest):
        return pl.ds(pl.multiple_of(lax.rem(dest, 4) * 256, 256), 256)

    def load_q(dest, sub, part, step, di, width=256, first=0):
        shard = lax.div(dest, 4)
        left = tok_all[2 * xh + shard, :, columns(dest)]
        left_other = tok_other[shard, :, columns(dest)]
        if part is not None:
            left = left[:, part * 128 : (part + 1) * 128]
            left_other = left_other[:, part * 128 : (part + 1) * 128]
        cut = slice(first + sub * width, first + (sub + 1) * width)
        return dot(left, gqkv[0, :, cut], 0, 0) + dot(left_other, gqkv[1, :, cut], 0, 0)

    def done_q(sub, value):
        cut = pl.ds(sub * 256, 256)
        gwq[sub] = value.astype(BF16)
        store(gwq.at[sub], gwq_hbm.at[:, cut])

    ring_q = scatter_ring(place, (0, 1), 256, load_q, q_sb, q_rb, send_sem, q_rs, sends, done_q)

    def load_k(dest, sub, part, step, di):
        return load_q(dest, sub, part, step, di, 128, 512)

    def done_k(sub, value):
        cut = pl.ds(sub * 128, 128)
        gwq[2, :, cut] = value.astype(BF16)
        store(gwq.at[2, :, cut], gwq_hbm.at[:, pl.ds(512 + sub * 128, 128)])

    ring_k = scatter_ring(place, (0, 1), 256, load_k, k_sb, k_rb, send_sem, k_rs, sends, done_k)

    def squeeze(value, column):
        e = expo[:, column : column + 1]
        sent = jnp.clip(value * jnp.exp2(-e), -127.0, 127.0).astype(BF16)
        return sent.astype(F32) * jnp.exp2(e)

    share_start()
    backward(0, around(4))
    backward(1, around(3))
    backward(2, around(-3))
    backward(3, around(2))
    step_merged(0)
    backward(4, around(-2))
    backward(5, around(1))
    step_merged(1)
    backward(6, around(-1))
    backward(7, z)
    grad = dq[...].T * SCALE
    x_gq = []
    for h in range(QUERY_PER_KEY):
        gqkv[0, :, h * HEAD_SIZE : (h + 1) * HEAD_SIZE] = turn(
            squeeze(grad[h * ROWS : (h + 1) * ROWS], h), c, -s
        ).astype(BF16)
        if h % 2:
            cut = pl.ds((h - 1) * HEAD_SIZE, 2 * HEAD_SIZE)
            sem = (4, 15)[h // 2]
            x_gq.append(swap(gqkv.at[0, :, cut], gqkv.at[1, :, cut], sem))
    step_merged(0)
    ring_kv.far()
    step_merged(1)
    cross_start(attended_term, att_s, att_r, 3)
    ring_kv.middle()
    step_merged(0)
    step_merged(1)
    ring_kv.near()
    for copy in x_tok:
        copy.wait_recv()
    share_forward()
    cross_forward(attended_term, att_s, att_r, 3)
    x_gq[0].wait_recv()
    run(ring_q, 1)
    x_gq[1].wait_recv()
    run(ring_q, 1)
    kv_sum = ring_kv.end()
    gqkv[0, :, 512:640] = turn(squeeze(kv_sum[:ROWS], 4), c, -s).astype(BF16)
    gqkv[0, :, 640:768] = squeeze(kv_sum[ROWS:], 5).astype(BF16)
    x_gkv = swap(gqkv.at[0, :, pl.ds(512, 256)], gqkv.at[1, :, pl.ds(512, 256)], 5)

    def tokens_term(dest):
        return dot(gqkv[0], wq[pl.ds(pl.multiple_of(dest * WIDTH, WIDTH), WIDTH)], 1, 1)

    cross_start(tokens_term, tok_s, tok_r, 4)
    att_own[...] = attended_term(t)
    run(ring_q, 2)
    x_gkv.wait_recv()
    run(ring_k, 2)
    for ring in merged_rings:
        run(ring)
    share_end()

    def out_term(h, column):
        tokens = NZ * ROWS
        return dot(
            merged_all[h].reshape(tokens, 256), slab[column].reshape(tokens, 256), 0, 0
        )

    for h in range(2):
        o_sb[pl.ds(h * 256, 256)] = out_term(h, 1 - xh).astype(BF16)
    x_o = swap(o_sb, o_rb, 3)
    tok_own[...] = tokens_term(t)
    run(ring_q, 2)
    run(ring_k, 2)
    cross_forward(tokens_term, tok_s, tok_r, 4)
    run(ring_k, 2)
    run(ring_q, 2)
    cross_end(att_own, att_r, 3, attended)
    store(attended, attended_hbm)
    run(ring_k, 2)
    run(ring_q)
    x_o.wait_recv()
    for h in range(2):
        rows = pl.ds(h * 256, 256)
        gwo[rows] = (out_term(h, xh) + o_rb[rows]).astype(BF16)
    store(gwo, gwo_hbm)
    cross_end(tok_own, tok_r, 4, grad_tokens)
    store(grad_tokens, grad_tokens_hbm)
    run(ring_k)
    pieces_sent()

    @pl.when(xh == 1)
    def _():
        for slot in range(NZ):
            give_dkv(slot).wait_send()

    share_sent()
    for copy in sends:
        copy.wait_send()
    for copy in stores:
        copy.wait()


def layer(tok, up, wq, wo, freqs, exponents):
    vmem = pl.BlockSpec(memory_space=pltpu.VMEM)
    hbm = pl.BlockSpec(memory_space=pl.ANY)
    shape = jax.ShapeDtypeStruct
    dma = pltpu.SemaphoreType.DMA
    buf = pltpu.VMEM
    heads = QUERY_PER_KEY * HEAD_SIZE
    return pl.pallas_call(
        layer_kernel,
        name="layer",
        out_shape=[
            shape((ROWS, WIDTH), BF16),
            shape((ROWS, WIDTH), BF16),
            shape((256, 768), BF16),
            shape((512, 256), BF16),
        ],
        in_specs=[hbm, hbm, hbm, hbm, vmem, vmem],
        out_specs=[hbm] * 4,
        scratch_shapes=[
            buf(wq.shape, BF16),
            buf(wo.shape, BF16),
            buf((NT, ROWS, WIDTH), BF16),
            buf((NT, ROWS, WIDTH), BF16),
            buf((2, ROWS, WIDTH), BF16),
            buf((2, NZ, ROWS, 256), BF16),
            buf((ROWS, HEAD_SIZE), F32),
            buf((ROWS, HEAD_SIZE), F32),
            buf((ROWS, 6), F32),
            buf((QROWS, HEAD_SIZE), BF16),
            buf((2, NZ, PAIR, HEAD_SIZE), BF16),
            buf((QROWS, HEAD_SIZE), BF16),
            buf((ROWS, heads), BF16),
            buf((2, NZ, ROWS, 256), BF16),
            buf((2, ROWS, 768), BF16),
            buf((PAIR, HEAD_SIZE), jnp.int32),
            buf((1, QROWS), jnp.int32),
            buf((1, QROWS), F32),
            buf((1, QROWS), F32),
            buf((HEAD_SIZE, QROWS), F32),
            buf((1, QROWS), F32),
            buf((1, QROWS), F32),
            buf((HEAD_SIZE, QROWS), F32),
            buf((NZ, 2, PAIR, HEAD_SIZE), BF16),
            buf((NZ, PAIR, HEAD_SIZE), BF16),
            buf((ROWS, WIDTH), F32),
            buf((3, ROWS, WIDTH), BF16),
            buf((3, ROWS, WIDTH), BF16),
            buf((ROWS, WIDTH), F32),
            buf((3, ROWS, WIDTH), BF16),
            buf((3, ROWS, WIDTH), BF16),
            buf((2, 4, PAIR, HEAD_SIZE), BF16),
            buf((2, 4, PAIR, HEAD_SIZE), BF16),
            buf((512, 256), BF16),
            buf((512, 256), BF16),
            buf((2, 4, 2, 256, 256), BF16),
            buf((2, 4, 2, 256, 256), BF16),
            buf((2, 4, 2, 256, 128), BF16),
            buf((2, 4, 2, 256, 128), BF16),
            buf((ROWS, WIDTH), BF16),
            buf((ROWS, WIDTH), BF16),
            buf((3, 256, 256), BF16),
            buf((512, 256), BF16),
            dma((7,)),
            dma((7,)),
            dma((1,)),
            dma((5, 6)),
            dma((16,)),
            dma((4, 2, 4)),
            dma((2, 4)),
            dma((2, 2, 4)),
            dma((NZ,)),
            dma((2, 4, 2)),
            dma((2, 4, 2)),
        ],
        compiler_params=pltpu.CompilerParams(
            collective_id=0, has_side_effects=True, vmem_limit_bytes=VMEM_LIMIT
        ),
    )(tok, up, wq, wo, freqs, exponents)


def settle_kernel(*refs):
    number = (len(refs) - 1) // 3
    sources, targets, held, sems = (
        refs[:number],
        refs[number : 2 * number],
        refs[2 * number : 3 * number],
        refs[-1],
    )
    for i in range(number):
        pltpu.make_async_copy(sources[i], held[i], sems.at[0, i]).start()
    for i in range(number):
        pltpu.make_async_copy(sources[i], held[i], sems.at[0, i]).wait()
        pltpu.make_async_copy(held[i], targets[i], sems.at[1, i]).start()
    for i in range(number):
        pltpu.make_async_copy(held[i], targets[i], sems.at[1, i]).wait()


def settle(*arrays):
    hbm = pl.BlockSpec(memory_space=pl.ANY)
    return pl.pallas_call(
        settle_kernel,
        name="settle",
        out_shape=[jax.ShapeDtypeStruct(a.shape, a.dtype) for a in arrays],
        in_specs=[hbm] * len(arrays),
        out_specs=[hbm] * len(arrays),
        scratch_shapes=[pltpu.VMEM(a.shape, a.dtype) for a in arrays]
        + [pltpu.SemaphoreType.DMA((2, len(arrays)))],
        compiler_params=pltpu.CompilerParams(vmem_limit_bytes=VMEM_LIMIT),
    )(*arrays)


def local(tokens, input_projection_weight, w_out, upstream, exponents):
    half = HEAD_SIZE // 2
    freqs = np.power(np.float32(THETA), -np.arange(half, dtype=np.float32) * 2.0 / HEAD_SIZE)
    freqs = jnp.asarray(np.tile(freqs, 2).reshape(1, HEAD_SIZE), F32)
    return settle(
        *layer(tokens, upstream, input_projection_weight, w_out, freqs, exponents.T)
    )


def solution(mesh):
    in_specs = (
        P(("dp", "seq"), "tensor"),
        P(None, "tensor"),
        P("tensor", None),
        P(("dp", "seq"), "tensor"),
        P("dp", "tensor"),
    )
    out_specs = (
        P(("dp", "seq"), "tensor"),
        P(("dp", "seq"), "tensor"),
        P(("dp", "seq"), "tensor"),
        P(("dp", "tensor"), "seq"),
    )
    return jax.shard_map(local, mesh=mesh, in_specs=in_specs, out_specs=out_specs, check_vma=False)
```

```python
import functools
import math

import jax
import jax.numpy as jnp
import numpy as np
from jax import lax
from jax.experimental import pallas as pl
from jax.experimental.pallas import tpu as pltpu
from jax.sharding import PartitionSpec as P

HEAD_SIZE = 128
QUERY_PER_KEY = 4
SCALE_TOKENS = 16
THETA = 500000.0

NZ = 8
NT = 4
ROWS = 192
QROWS = QUERY_PER_KEY * ROWS
PAIR = 2 * ROWS
WIDTH = 1024
MESH = pl.DeviceIdType.MESH
BF16 = jnp.bfloat16
F32 = jnp.float32
SCALE = 1.0 / math.sqrt(HEAD_SIZE)
SCALE2 = SCALE * math.log2(math.e)
VMEM_LIMIT = 60 * 2**20


def dot(left, right, left_dim, right_dim):
    return lax.dot_general(
        left, right, (((left_dim,), (right_dim,)), ((), ())), preferred_element_type=F32
    )


class Place:
    def __init__(self):
        self.d = lax.axis_index("dp")
        self.s = lax.axis_index("seq")
        self.t = lax.axis_index("tensor")
        self.xh = lax.div(self.s, NZ)
        self.z = lax.rem(self.s, NZ)

    def tensor(self, offset):
        return (self.d, self.s, lax.rem(self.t + offset, NT))

    def zdev(self, sign):
        return (self.d, self.xh * NZ + lax.rem(self.z + sign + NZ, NZ), self.t)

    def xdev(self):
        return (self.d, (1 - self.xh) * NZ + self.z, self.t)

    def diagonal(self, sign):
        return (self.d, (1 - self.xh) * NZ + lax.rem(self.z + sign + NZ, NZ), self.t)

    def enter(self):
        barrier = pltpu.get_barrier_semaphore()
        partners = [self.tensor(1), self.tensor(3)]
        partners += [self.zdev(i) for i in range(1, NZ)] + [self.xdev()]
        partners += [self.diagonal(1), self.diagonal(-1)]
        for partner in partners:
            pl.semaphore_signal(barrier, inc=1, device_id=partner, device_id_type=MESH)
        pl.semaphore_wait(barrier, len(partners))


def remote(src, dst, send_sem, recv_sem, device):
    return pltpu.make_async_remote_copy(
        src_ref=src,
        dst_ref=dst,
        send_sem=send_sem,
        recv_sem=recv_sem,
        device_id=device,
        device_id_type=MESH,
    )


def turn(vectors, cosine, sine):
    return vectors * cosine + pltpu.roll(vectors, HEAD_SIZE // 2, 1) * sine


def gather_ring(place, part, which, ss, rs, sends, first=1):
    def arrived(step, di, sign):
        ref = part(step, di, place.z - sign * step)
        sem = rs.at[which, di, step - 1]
        remote(ref, ref, ss.at[0], sem, place.zdev(sign)).wait_recv()

    for step in range(first, 5):
        for di, sign in ((0, 1), (1, -1)):
            if step > 1:
                arrived(step - 1, di, sign)
            ref = part(step, di, place.z - sign * (step - 1))
            copy = remote(
                ref,
                ref,
                ss.at[0],
                rs.at[which, di, step - 1],
                place.zdev(sign),
            )
            copy.start()
            sends.append(copy)
        yield
    for di, sign in ((0, 1), (1, -1)):
        arrived(4, di, sign)


def scatter_ring(place, subs, rows, load, sbuf, rbuf, ss, rs, sends, done):
    half = rows // 2
    for step in (4, 3, 2, 1):
        for sub in subs:
            for di, sign in ((0, 1), (1, -1)):
                dest = lax.rem(place.z + sign * step + NZ, NZ)
                cut = pl.ds(di * half, half)
                here = sbuf.at[di, step - 1, sub]
                there = rbuf.at[di, step - 1, sub]
                if step == 4:
                    here, there = here.at[cut], there.at[cut]
                    here[...] = load(dest, sub, di, step, di).astype(BF16)
                else:
                    value = load(dest, sub, None, step, di)
                    before = rbuf.at[di, step, sub]
                    if step == 3:
                        before = before.at[cut]
                    remote(
                        before, before, ss.at[0], rs.at[di, step, sub], place.zdev(sign)
                    ).wait_recv()
                    if step == 3:
                        here[cut] = (value[di * half : (di + 1) * half] + before[...]).astype(BF16)
                        rest = 1 - di
                        here[pl.ds(rest * half, half)] = value[
                            rest * half : (rest + 1) * half
                        ].astype(BF16)
                    else:
                        here[...] = (value + before[...]).astype(BF16)
                copy = remote(
                    here, there, ss.at[0], rs.at[di, step - 1, sub], place.zdev(sign)
                )
                copy.start()
                sends.append(copy)
            yield
    for sub in subs:
        total = load(place.z, sub, None, 0, 0)
        for di, sign in ((0, 1), (1, -1)):
            ref = rbuf.at[di, 0, sub]
            remote(ref, ref, ss.at[0], rs.at[di, 0, sub], place.zdev(sign)).wait_recv()
            total = total + ref[...]
        done(sub, total)


def run(steps, count=None):
    if count is None:
        for _ in steps:
            pass
    else:
        for _ in range(count):
            next(steps)


class TwoStages:
    def __init__(self, place, rows, term, sbuf, rbuf, ss, rs, sends):
        self.place, self.half, self.term, self.sends = place, rows // 2, term, sends
        self.refs = sbuf, rbuf, ss, rs

    def copy(self, di, step, hops):
        sbuf, rbuf, ss, rs = self.refs
        at = (di, step - 1)
        here, there = sbuf.at[at], rbuf.at[at]
        if step == 4:
            cut = pl.ds(di * self.half, self.half)
            here, there = here.at[cut], there.at[cut]
        return remote(here, there, ss.at[0], rs.at[at], self.place.zdev(hops))

    def send(self, di, step, hops, value):
        sbuf = self.refs[0]
        if step == 4:
            cut = slice(di * self.half, (di + 1) * self.half)
            sbuf[di, step - 1, cut] = value[cut].astype(BF16)
        else:
            sbuf[di, step - 1] = value.astype(BF16)
        copy = self.copy(di, step, hops)
        copy.start()
        self.sends.append(copy)

    def far(self):
        value = self.term(4, 0)
        for di, sign in ((0, 1), (1, -1)):
            self.send(di, 3, sign, self.term(3, di))
            self.send(di, 4, 2 * sign, value)

    def near(self):
        for di, sign in ((0, 1), (1, -1)):
            self.send(di, 1, sign, self.term(1, di))

    def middle(self):
        half, (_, rbuf, _, _) = self.half, self.refs
        for di, sign in ((0, 1), (1, -1)):
            value = self.term(2, di)
            self.copy(di, 3, sign).wait_recv()
            self.copy(di, 4, 2 * sign).wait_recv()
            value = value + rbuf[di, 2]
            parts = [value[:half], value[half:]]
            parts[di] = parts[di] + rbuf[di, 3, di * half : (di + 1) * half]
            self.send(di, 2, 2 * sign, jnp.concatenate(parts, axis=0))

    def end(self):
        value = self.term(0, 0)
        for di, sign in ((0, 1), (1, -1)):
            for step in (1, 2):
                self.copy(di, step, step * sign).wait_recv()
                value = value + self.refs[1][di, step - 1]
        return value


def layer_kernel(
    tok_hbm, up_hbm, wq_hbm, wo_hbm, freqs, exponents,
    attended_hbm, grad_tokens_hbm, gwq_hbm, gwo_hbm,
    wq, wo, tok_all, up_all, tok_other, slab, cosine, sine, expo,
    q, kv, do, merged, merged_all, gqkv,
    key_place, limit, top, total, acc, logsum, delta, dq,
    dkv, dkv_other,
    att_own, att_s, att_r, tok_own, tok_s, tok_r,
    kv_sb, kv_rb, o_sb, o_rb, q_sb, q_rb, k_sb, k_rb,
    attended, grad_tokens, gwq, gwo,
    load_sem, store_sem, send_sem, y_rs, x_rs, ag_rs,
    kv_rs, m_rs, a_rs, q_rs, k_rs,
):
    place = Place()
    t, xh, z = place.t, place.xh, place.z
    tok, up = tok_all.at[t], up_all.at[t]
    load_tok = pltpu.make_async_copy(tok_hbm, tok, load_sem.at[5])
    load_tok.start()
    load_up = pltpu.make_async_copy(up_hbm, up, load_sem.at[6])
    load_up.start()
    loads = []
    for i in range(NT):
        rows = pl.ds(pl.multiple_of(lax.rem(t + (0, 1, 3, 2)[i], NT) * WIDTH, WIDTH), WIDTH)
        loads.append(pltpu.make_async_copy(wq_hbm.at[rows], wq.at[rows], load_sem.at[i]))
        loads[-1].start()
    load_wo = pltpu.make_async_copy(wo_hbm, wo, load_sem.at[4])
    load_wo.start()
    place.enter()
    sends = []
    half = ROWS // 2

    def swap(src, dst, i):
        copy = remote(src, dst, send_sem.at[0], x_rs.at[i], place.xdev())
        copy.start()
        sends.append(copy)
        return copy

    def on_y(src, dst, which, i, offset):
        return remote(src, dst, send_sem.at[0], y_rs.at[which, i], place.tensor(offset))

    before, after, across = (lax.rem(t + i, NT) for i in (3, 1, 2))

    def halves(first, rows):
        return pl.ds(first, rows // 2), pl.ds(first + rows // 2, rows // 2)

    def tensor_start(everyone, which):
        for rest in range(2):
            for i, offset in ((0, 1), (1, 3)):
                ref = everyone.at[t, halves(0, ROWS)[(i + rest) % 2]]
                copy = on_y(ref, ref, which, i + 4 * rest, offset)
                copy.start()
                sends.append(copy)

    def tensor_forward(everyone, which):
        for i, offset, source in ((0, 1, before), (1, 3, after)):
            ref = everyone.at[source, halves(0, ROWS)[i]]
            on_y(ref, ref, which, i, offset).wait_recv()
            copy = on_y(ref, ref, which, 2 + i, offset)
            copy.start()
            sends.append(copy)

    def tensor_rest(everyone, which):
        for i, offset, source in ((0, 1, before), (1, 3, after)):
            ref = everyone.at[source, halves(0, ROWS)[1 - i]]
            on_y(ref, ref, which, 4 + i, offset).wait_recv()

    def tensor_end(everyone, which):
        for i, offset in ((0, 1), (1, 3)):
            ref = everyone.at[across, halves(0, ROWS)[i]]
            on_y(ref, ref, which, 2 + i, offset).wait_recv()

    def holder(source):
        return lax.rem(source, 2) == lax.div(z, 4)

    def piece(i):
        dest = 4 * lax.rem(t, 2) + i
        target = slab.at[lax.div(t, 2), z]
        source = up.at[:, pl.ds(i * 256, 256)]
        device = (place.d, xh * NZ + dest, t)
        return dest, source, remote(source, target, send_sem.at[0], a_rs.at[z], device)

    def spread_pieces():
        for i in range(4):
            dest, source, copy = piece(i)

            @pl.when(dest != z)
            def _(copy=copy):
                copy.start()

            @pl.when(dest == z)
            def _(source=source):
                slab[lax.div(t, 2), z] = source[...]

    def pieces_sent():
        for i in range(4):
            dest, _, copy = piece(i)

            @pl.when(dest != z)
            def _(copy=copy):
                copy.wait_send()

    def slab_half(source, i):
        return slab.at[lax.div(source, 2), pl.ds(4 * i, 4)]

    def share_start():
        @pl.when(holder(t))
        def _():
            for i in range(1, NZ):
                source = lax.rem(z + i, NZ)
                ref = slab.at[lax.div(t, 2), source]
                remote(ref, ref, send_sem.at[0], a_rs.at[source], place.zdev(1)).wait_recv()
            ref = slab.at[lax.div(t, 2)]
            on_y(ref, ref, 2, 0, 1).start()
            on_y(ref, ref, 2, 1, 3).start()

    def share_forward():
        @pl.when(holder(before))
        def _():
            for i, offset, source in ((0, 1, before), (1, 3, after)):
                ref = slab.at[lax.div(source, 2)]
                on_y(ref, ref, 2, i, offset).wait_recv()
                ref = slab_half(source, i)
                on_y(ref, ref, 2, 2 + i, offset).start()

    def share_end():
        @pl.when(holder(across))
        def _():
            for i, offset in ((0, 1), (1, 3)):
                ref = slab_half(across, i)
                on_y(ref, ref, 2, 2 + i, offset).wait_recv()

    def share_sent():
        @pl.when(holder(t))
        def _():
            ref = slab.at[lax.div(t, 2)]
            on_y(ref, ref, 2, 0, 1).wait_send()
            on_y(ref, ref, 2, 1, 3).wait_send()

        @pl.when(holder(before))
        def _():
            for i, offset, source in ((0, 1, before), (1, 3, after)):
                ref = slab_half(source, i)
                on_y(ref, ref, 2, 2 + i, offset).wait_send()

    stores = []

    def store(src, dst):
        copy = pltpu.make_async_copy(src, dst, store_sem.at[len(stores)])
        copy.start()
        stores.append(copy)

    def cross_start(term, sbuf, rbuf, which):
        value = term(across).astype(BF16)
        for i, offset in ((0, 1), (1, 3)):
            part = halves(0, ROWS)[i]
            sbuf[0, part] = value[i * half : (i + 1) * half]
            copy = on_y(sbuf.at[0, part], rbuf.at[0, part], which, 2 + i, offset)
            copy.start()
            sends.append(copy)

    def cross_forward(term, sbuf, rbuf, which):
        for i, offset, dest in ((0, 1, after), (1, 3, before)):
            value = term(dest)
            part = halves(0, ROWS)[i]
            ref = rbuf.at[0, part]
            on_y(ref, ref, which, 2 + i, offset).wait_recv()
            rest = slice((1 - i) * half, (2 - i) * half)
            sbuf[1 + i, part] = (value[i * half : (i + 1) * half] + ref[...]).astype(BF16)
            sbuf[1 + i, halves(0, ROWS)[1 - i]] = value[rest].astype(BF16)
            copy = on_y(sbuf.at[1 + i], rbuf.at[1 + i], which, i, offset)
            copy.start()
            sends.append(copy)

    def cross_end(own, rbuf, which, out):
        value = own[...]
        for i, offset in ((0, 1), (1, 3)):
            ref = rbuf.at[1 + i]
            on_y(ref, ref, which, i, offset).wait_recv()
            value = value + ref[...]
        out[...] = value.astype(BF16)

    load_tok.wait()
    tensor_start(tok_all, 0)
    load_up.wait()
    spread_pieces()
    position = lax.broadcasted_iota(jnp.int32, (ROWS, HEAD_SIZE), 0) + place.s * ROWS
    angles = position.astype(F32) * freqs[...]
    cosine[...] = jnp.cos(angles)
    low = lax.broadcasted_iota(jnp.int32, (ROWS, HEAD_SIZE), 1) < HEAD_SIZE // 2
    sines = jnp.sin(angles)
    sine[...] = jnp.where(low, -sines, sines)
    groups = exponents.shape[1]
    group = lax.broadcasted_iota(jnp.int32, (ROWS, groups), 0) // SCALE_TOKENS
    group = group + place.s * (ROWS // SCALE_TOKENS)
    pick = lax.broadcasted_iota(jnp.int32, (ROWS, groups), 1) == group
    expo[...] = dot(pick.astype(F32).astype(BF16), exponents[...].astype(F32).astype(BF16), 1, 1)
    row = lax.broadcasted_iota(jnp.int32, (PAIR, HEAD_SIZE), 0)
    key_place[...] = jnp.where(row < ROWS, row, row + (NZ - 1) * ROWS)
    limit[...] = place.s * ROWS + lax.rem(
        lax.broadcasted_iota(jnp.int32, (1, QROWS), 1), jnp.int32(ROWS)
    )
    top[...] = jnp.full(top.shape, -jnp.inf, F32)
    total[...] = jnp.zeros(total.shape, F32)
    acc[...] = jnp.zeros(acc.shape, F32)
    dq[...] = jnp.zeros(dq.shape, F32)

    @pl.when(xh == 1)
    def _():
        dkv_other[...] = jnp.zeros(dkv_other.shape, BF16)

    def weight_rows(source):
        return pl.ds(pl.multiple_of(source * WIDTH, WIDTH), WIDTH)

    def project_kv(source):
        return dot(tok_all[source], wq[weight_rows(source), 512:768], 1, 0)

    def project_q(source):
        return dot(tok_all[source], wq[weight_rows(source), 0:512], 1, 0)

    def around(step):
        return lax.rem(z + step + NZ, NZ)

    def forward(zk):
        keys = kv[0, zk]
        values = kv[1, zk]
        for cut in range(0, QROWS, HEAD_SIZE):
            cut = slice(cut, cut + HEAD_SIZE)
            scores = dot(keys, q[cut], 1, 1)
            allowed = key_place[...] <= limit[:, cut] - zk * ROWS
            scores = jnp.where(allowed, scores, -jnp.inf)
            before = top[:, cut]
            now = jnp.maximum(before, jnp.max(scores, axis=0, keepdims=True))
            weights = jnp.exp2((scores - now) * SCALE2)
            alpha = jnp.exp2((before - now) * SCALE2)
            top[:, cut] = now
            total[:, cut] = total[:, cut] * alpha + jnp.sum(weights, axis=0, keepdims=True)
            acc[:, cut] = acc[:, cut] * alpha + dot(values, weights.astype(BF16), 0, 0)

    def merged_term(source):
        return dot(up_all[source], wo[:, weight_rows(source)], 1, 1)

    c, s = cosine[...], sine[...]

    def kv_part(column, i):
        def part(step, di, at):
            first = column * ROWS
            rows = pl.ds(pl.multiple_of(first, ROWS), ROWS)
            if step == 4:
                rows = pl.ds(pl.multiple_of(first + di * half, half), half)
            return kv.at[i, lax.rem(at + 2 * NZ, NZ), rows]

        return part

    own_rings = [gather_ring(place, kv_part(xh, i), i, send_sem, ag_rs, sends) for i in range(2)]
    other_rings = [
        gather_ring(place, kv_part(1 - xh, i), 2 + i, send_sem, ag_rs, sends, 2) for i in range(2)
    ]

    def step_kv(i):
        run(own_rings[i], 1)
        run(other_rings[i], 1)

    for load in loads:
        load.wait()
    projected = project_kv(t)
    tensor_forward(tok_all, 0)
    tensor_rest(tok_all, 0)
    projected = projected + project_kv(before) + project_kv(after)
    tensor_end(tok_all, 0)
    tensor_start(up_all, 1)
    projected = projected + project_kv(across)
    rows = pl.ds(pl.multiple_of(xh * ROWS, ROWS), ROWS)
    kv[0, z, rows] = turn(projected[:, 0:128], c, s).astype(BF16)
    kv[1, z, rows] = projected[:, 128:256].astype(BF16)
    for i in range(2):
        own = kv.at[i, z, rows]
        run(own_rings[i], 1)
        for di, sign in ((0, 1), (1, -1)):
            copy = remote(
                own, own, send_sem.at[0], ag_rs.at[2 + i, di, 0], place.diagonal(sign)
            )
            copy.start()
            sends.append(copy)
        swap(own, own, (0, 14)[i])
    projected = project_q(t) + project_q(before) + project_q(after) + project_q(across)
    for h in range(QUERY_PER_KEY):
        q[pl.ds(h * ROWS, ROWS)] = turn(
            projected[:, h * HEAD_SIZE : (h + 1) * HEAD_SIZE], c, s
        ).astype(BF16)
    x_tok = [swap(tok_all.at[2 * (1 - xh) + i], tok_other.at[i], 1 + i) for i in range(2)]
    step_kv(0)
    step_kv(1)
    for i in range(2):
        other = kv_part(1 - xh, i)(1, 0, z)
        sem = (0, 14)[i]
        remote(other, other, send_sem.at[0], x_rs.at[sem], place.xdev()).wait_recv()
    forward(z)
    forward(around(1))
    step_kv(0)
    forward(around(-1))
    step_kv(1)
    forward(around(2))
    tensor_forward(up_all, 1)
    tensor_rest(up_all, 1)
    load_wo.wait()
    grad = merged_term(t) + merged_term(before)
    step_kv(0)
    forward(around(-2))
    step_kv(1)
    forward(around(3))
    grad = grad + merged_term(after)
    run(own_rings[0])
    run(other_rings[0])
    forward(around(-3))
    run(own_rings[1])
    run(other_rings[1])
    forward(around(4))

    out_t = (acc[...] / total[...]).astype(BF16)
    out = out_t.astype(F32).T.astype(BF16)
    for h in range(QUERY_PER_KEY):
        rows = out[h * ROWS : (h + 1) * ROWS]
        merged[:, h * HEAD_SIZE : (h + 1) * HEAD_SIZE] = rows
        merged_all[h // 2, z, :, (h % 2) * HEAD_SIZE : (h % 2 + 1) * HEAD_SIZE] = rows

    def merged_part(h):
        def part(step, di, at):
            ref = merged_all.at[h, lax.rem(at + 2 * NZ, NZ)]
            return ref.at[pl.ds(di * (ROWS // 2), ROWS // 2)] if step == 4 else ref

        return part

    merged_rings = [
        gather_ring(place, merged_part(h), h, send_sem, m_rs, sends) for h in range(2)
    ]

    def step_merged(h):
        run(merged_rings[h], 1)

    step_merged(0)
    step_merged(1)
    tensor_end(up_all, 1)
    grad = grad + merged_term(across)
    for h in range(QUERY_PER_KEY):
        do[pl.ds(h * ROWS, ROWS)] = grad[:, h * HEAD_SIZE : (h + 1) * HEAD_SIZE].astype(BF16)
    logsum[...] = top[...] * SCALE2 + jnp.log2(total[...])
    delta[...] = jnp.sum(do[...].astype(F32).T * out_t.astype(F32), axis=0, keepdims=True)

    def give_dkv(slot):
        return remote(
            dkv.at[slot, 0], dkv_other.at[slot], send_sem.at[0], x_rs.at[6 + slot], place.xdev()
        )

    def cross_dkv(slot):
        @pl.when(xh == 1)
        def _():
            give_dkv(slot).start()

    def backward(slot, zk):
        keys = kv[0, zk]
        values = kv[1, zk]
        scores = dot(keys, q[...], 1, 1)
        allowed = key_place[:, 0:1] <= limit[...] - zk * ROWS
        probs = jnp.exp2(jnp.where(allowed, scores * SCALE2 - logsum[...], -jnp.inf))
        grad_probs = dot(values, do[...], 1, 1)
        grad_scores = (probs * (grad_probs - delta[...])).astype(BF16)
        dv = dot(probs.astype(BF16), do[...], 1, 0).astype(BF16)
        dk = (dot(grad_scores, q[...], 1, 0) * SCALE).astype(BF16)
        dq[...] += dot(keys, grad_scores, 0, 0)
        for column in range(2):
            rows = slice(column * ROWS, (column + 1) * ROWS)
            dkv[slot, column, 0:ROWS] = dk[rows]
            dkv[slot, column, ROWS:PAIR] = dv[rows]
        cross_dkv(slot)

    kv_here = set()

    def kv_term(step, di):
        slot = {4: 0, 3: 1, 2: 3, 1: 5, 0: 7}[step] + (di if step in (1, 2, 3) else 0)
        if slot not in kv_here:
            kv_here.add(slot)

            @pl.when(xh == 0)
            def _():
                give_dkv(slot).wait_recv()

        return dkv[slot, xh].astype(F32) + dkv_other[slot].astype(F32)

    ring_kv = TwoStages(place, PAIR, kv_term, kv_sb, kv_rb, send_sem, kv_rs, sends)

    def attended_term(dest):
        return dot(merged[...], wo[:, pl.ds(pl.multiple_of(dest * WIDTH, WIDTH), WIDTH)], 1, 0)

    def columns(dest):
        return pl.ds(pl.multiple_of(lax.rem(dest, 4) * 256, 256), 256)

    def load_q(dest, sub, part, step, di, width=256, first=0):
        shard = lax.div(dest, 4)
        left = tok_all[2 * xh + shard, :, columns(dest)]
        left_other = tok_other[shard, :, columns(dest)]
        if part is not None:
            left = left[:, part * 128 : (part + 1) * 128]
            left_other = left_other[:, part * 128 : (part + 1) * 128]
        cut = slice(first + sub * width, first + (sub + 1) * width)
        return dot(left, gqkv[0, :, cut], 0, 0) + dot(left_other, gqkv[1, :, cut], 0, 0)

    def done_q(sub, value):
        cut = pl.ds(sub * 256, 256)
        gwq[sub] = value.astype(BF16)
        store(gwq.at[sub], gwq_hbm.at[:, cut])

    ring_q = scatter_ring(place, (0, 1), 256, load_q, q_sb, q_rb, send_sem, q_rs, sends, done_q)

    def load_k(dest, sub, part, step, di):
        return load_q(dest, sub, part, step, di, 128, 512)

    def done_k(sub, value):
        cut = pl.ds(sub * 128, 128)
        gwq[2, :, cut] = value.astype(BF16)
        store(gwq.at[2, :, cut], gwq_hbm.at[:, pl.ds(512 + sub * 128, 128)])

    ring_k = scatter_ring(place, (0, 1), 256, load_k, k_sb, k_rb, send_sem, k_rs, sends, done_k)

    def squeeze(value, column):
        e = expo[:, column : column + 1]
        sent = jnp.clip(value * jnp.exp2(-e), -127.0, 127.0).astype(BF16)
        return sent.astype(F32) * jnp.exp2(e)

    share_start()
    backward(0, around(4))
    backward(1, around(3))
    backward(2, around(-3))
    backward(3, around(2))
    step_merged(0)
    backward(4, around(-2))
    backward(5, around(1))
    step_merged(1)
    backward(6, around(-1))
    backward(7, z)
    grad = dq[...].T * SCALE
    x_gq = []
    for h in range(QUERY_PER_KEY):
        gqkv[0, :, h * HEAD_SIZE : (h + 1) * HEAD_SIZE] = turn(
            squeeze(grad[h * ROWS : (h + 1) * ROWS], h), c, -s
        ).astype(BF16)
        if h % 2:
            cut = pl.ds((h - 1) * HEAD_SIZE, 2 * HEAD_SIZE)
            sem = (4, 15)[h // 2]
            x_gq.append(swap(gqkv.at[0, :, cut], gqkv.at[1, :, cut], sem))
    step_merged(0)
    ring_kv.far()
    step_merged(1)
    cross_start(attended_term, att_s, att_r, 3)
    ring_kv.middle()
    step_merged(0)
    step_merged(1)
    ring_kv.near()
    for copy in x_tok:
        copy.wait_recv()
    share_forward()
    cross_forward(attended_term, att_s, att_r, 3)
    x_gq[0].wait_recv()
    run(ring_q, 1)
    x_gq[1].wait_recv()
    run(ring_q, 1)
    kv_sum = ring_kv.end()
    gqkv[0, :, 512:640] = turn(squeeze(kv_sum[:ROWS], 4), c, -s).astype(BF16)
    gqkv[0, :, 640:768] = squeeze(kv_sum[ROWS:], 5).astype(BF16)
    x_gkv = swap(gqkv.at[0, :, pl.ds(512, 256)], gqkv.at[1, :, pl.ds(512, 256)], 5)

    def tokens_term(dest):
        return dot(gqkv[0], wq[pl.ds(pl.multiple_of(dest * WIDTH, WIDTH), WIDTH)], 1, 1)

    cross_start(tokens_term, tok_s, tok_r, 4)
    att_own[...] = attended_term(t)
    run(ring_q, 2)
    x_gkv.wait_recv()
    run(ring_k, 2)
    for ring in merged_rings:
        run(ring)
    share_end()

    def out_term(h, column):
        tokens = NZ * ROWS
        return dot(
            merged_all[h].reshape(tokens, 256), slab[column].reshape(tokens, 256), 0, 0
        )

    for h in range(2):
        o_sb[pl.ds(h * 256, 256)] = out_term(h, 1 - xh).astype(BF16)
    x_o = swap(o_sb, o_rb, 3)
    tok_own[...] = tokens_term(t)
    run(ring_q, 2)
    run(ring_k, 2)
    cross_forward(tokens_term, tok_s, tok_r, 4)
    run(ring_k, 2)
    run(ring_q, 2)
    cross_end(att_own, att_r, 3, attended)
    store(attended, attended_hbm)
    run(ring_k, 2)
    run(ring_q)
    x_o.wait_recv()
    for h in range(2):
        rows = pl.ds(h * 256, 256)
        gwo[rows] = (out_term(h, xh) + o_rb[rows]).astype(BF16)
    store(gwo, gwo_hbm)
    cross_end(tok_own, tok_r, 4, grad_tokens)
    store(grad_tokens, grad_tokens_hbm)
    run(ring_k)
    pieces_sent()

    @pl.when(xh == 1)
    def _():
        for slot in range(NZ):
            give_dkv(slot).wait_send()

    share_sent()
    for copy in sends:
        copy.wait_send()
    for copy in stores:
        copy.wait()


def layer(tok, up, wq, wo, freqs, exponents):
    vmem = pl.BlockSpec(memory_space=pltpu.VMEM)
    hbm = pl.BlockSpec(memory_space=pl.ANY)
    shape = jax.ShapeDtypeStruct
    dma = pltpu.SemaphoreType.DMA
    buf = pltpu.VMEM
    heads = QUERY_PER_KEY * HEAD_SIZE
    return pl.pallas_call(
        layer_kernel,
        name="layer",
        out_shape=[
            shape((ROWS, WIDTH), BF16),
            shape((ROWS, WIDTH), BF16),
            shape((256, 768), BF16),
            shape((512, 256), BF16),
        ],
        in_specs=[hbm, hbm, hbm, hbm, vmem, vmem],
        out_specs=[hbm] * 4,
        scratch_shapes=[
            buf(wq.shape, BF16),
            buf(wo.shape, BF16),
            buf((NT, ROWS, WIDTH), BF16),
            buf((NT, ROWS, WIDTH), BF16),
            buf((2, ROWS, WIDTH), BF16),
            buf((2, NZ, ROWS, 256), BF16),
            buf((ROWS, HEAD_SIZE), F32),
            buf((ROWS, HEAD_SIZE), F32),
            buf((ROWS, 6), F32),
            buf((QROWS, HEAD_SIZE), BF16),
            buf((2, NZ, PAIR, HEAD_SIZE), BF16),
            buf((QROWS, HEAD_SIZE), BF16),
            buf((ROWS, heads), BF16),
            buf((2, NZ, ROWS, 256), BF16),
            buf((2, ROWS, 768), BF16),
            buf((PAIR, HEAD_SIZE), jnp.int32),
            buf((1, QROWS), jnp.int32),
            buf((1, QROWS), F32),
            buf((1, QROWS), F32),
            buf((HEAD_SIZE, QROWS), F32),
            buf((1, QROWS), F32),
            buf((1, QROWS), F32),
            buf((HEAD_SIZE, QROWS), F32),
            buf((NZ, 2, PAIR, HEAD_SIZE), BF16),
            buf((NZ, PAIR, HEAD_SIZE), BF16),
            buf((ROWS, WIDTH), F32),
            buf((3, ROWS, WIDTH), BF16),
            buf((3, ROWS, WIDTH), BF16),
            buf((ROWS, WIDTH), F32),
            buf((3, ROWS, WIDTH), BF16),
            buf((3, ROWS, WIDTH), BF16),
            buf((2, 4, PAIR, HEAD_SIZE), BF16),
            buf((2, 4, PAIR, HEAD_SIZE), BF16),
            buf((512, 256), BF16),
            buf((512, 256), BF16),
            buf((2, 4, 2, 256, 256), BF16),
            buf((2, 4, 2, 256, 256), BF16),
            buf((2, 4, 2, 256, 128), BF16),
            buf((2, 4, 2, 256, 128), BF16),
            buf((ROWS, WIDTH), BF16),
            buf((ROWS, WIDTH), BF16),
            buf((3, 256, 256), BF16),
            buf((512, 256), BF16),
            dma((7,)),
            dma((7,)),
            dma((1,)),
            dma((5, 6)),
            dma((16,)),
            dma((4, 2, 4)),
            dma((2, 4)),
            dma((2, 2, 4)),
            dma((NZ,)),
            dma((2, 4, 2)),
            dma((2, 4, 2)),
        ],
        compiler_params=pltpu.CompilerParams(
            collective_id=0, has_side_effects=True, vmem_limit_bytes=VMEM_LIMIT
        ),
    )(tok, up, wq, wo, freqs, exponents)


def settle_kernel(*refs):
    number = (len(refs) - 1) // 3
    sources, targets, held, sems = (
        refs[:number],
        refs[number : 2 * number],
        refs[2 * number : 3 * number],
        refs[-1],
    )
    for i in range(number):
        pltpu.make_async_copy(sources[i], held[i], sems.at[0, i]).start()
    for i in range(number):
        pltpu.make_async_copy(sources[i], held[i], sems.at[0, i]).wait()
        pltpu.make_async_copy(held[i], targets[i], sems.at[1, i]).start()
    for i in range(number):
        pltpu.make_async_copy(held[i], targets[i], sems.at[1, i]).wait()


def settle(*arrays):
    hbm = pl.BlockSpec(memory_space=pl.ANY)
    return pl.pallas_call(
        settle_kernel,
        name="settle",
        out_shape=[jax.ShapeDtypeStruct(a.shape, a.dtype) for a in arrays],
        in_specs=[hbm] * len(arrays),
        out_specs=[hbm] * len(arrays),
        scratch_shapes=[pltpu.VMEM(a.shape, a.dtype) for a in arrays]
        + [pltpu.SemaphoreType.DMA((2, len(arrays)))],
        compiler_params=pltpu.CompilerParams(vmem_limit_bytes=VMEM_LIMIT),
    )(*arrays)


def local(tokens, input_projection_weight, w_out, upstream, exponents):
    half = HEAD_SIZE // 2
    freqs = np.power(np.float32(THETA), -np.arange(half, dtype=np.float32) * 2.0 / HEAD_SIZE)
    freqs = jnp.asarray(np.tile(freqs, 2).reshape(1, HEAD_SIZE), F32)
    return settle(
        *layer(tokens, upstream, input_projection_weight, w_out, freqs, exponents.T)
    )


def solution(mesh):
    in_specs = (
        P(("dp", "seq"), "tensor"),
        P(None, "tensor"),
        P("tensor", None),
        P(("dp", "seq"), "tensor"),
        P("dp", "tensor"),
    )
    out_specs = (
        P(("dp", "seq"), "tensor"),
        P(("dp", "seq"), "tensor"),
        P(("dp", "seq"), "tensor"),
        P(("dp", "tensor"), "seq"),
    )
    return jax.shard_map(local, mesh=mesh, in_specs=in_specs, out_specs=out_specs, check_vma=False)
```
